256 devices in a mesh: branch: 4 (over y_lo, core), dp: 16 (over z, y_hi), mp: 4 (over x).
Axes of the slice: x: 4, y: 4 (y_hi: 2, y_lo: 2; y = y_hi * 2 + y_lo), z: 8, core: 2. Of those that a mesh axis runs over, the one named last changes fastest.
Arguments:
- context: bfloat16 [8192, 4096], P(('branch', 'dp')), may hold values from -6 to 6
- residual: bfloat16 [8192, 4096], P(('branch', 'dp')), may hold values from -40 to 40
- branch_out_proj: bfloat16 [4, 4096, 4096], P('branch', 'dp', 'mp'), may hold values from -0.09375 to 0.09375
- norm_gain: bfloat16 [4096], replicated, may hold values from 0.25 to 1.75
- router: bfloat16 [4096, 4], replicated, may hold values from -0.09375 to 0.09375
- expert_ids: int32 [8192, 2], P(('branch', 'dp')), may hold values from 0 to 3, all different within a row; in each aligned block of 128 rows (0 to 127, 128 to 255, ...) at most 72 rows name the same one
- gate_proj: bfloat16 [4, 4096, 6144], P('branch', None, 'dp'), may hold values from -0.09375 to 0.09375
- up_proj: bfloat16 [4, 4096, 6144], P('branch', None, 'dp'), may hold values from -0.09375 to 0.09375
- down_proj: bfloat16 [4, 6144, 4096], P('branch', 'dp'), may hold values from -0.078125 to 0.078125
Outputs:
- mixed: bfloat16 [8192, 4096], P(('branch', 'dp'))
The draws below stay inside these ranges and needn't reach their ends.
Inputs may be any that keep to these rules, and one draw needn't show every extreme that they name: `expert_ids`: among the rows of one device (aligned blocks of 128 rows), no expert is named by more than 72 rows; in some device one expert is named by exactly 72. A row names two different experts.
All inputs are finite; a program needn't handle non-finite values.
Results may differ from the reference program's by a relative error of at most 0.009.
Values may be sent and summed in bfloat16 or wider, within the bound.
A program may use at most 128 MiB of HBM per device.

```python
import math
import jax
import jax.numpy as jnp
import numpy as np
from jax import lax

D = 4096
FF = 6144
ROWS = 128
EXPERTS = 4
CAP = 72
FF_DEV = 384
TOKENS = 8192


def draw_residual(key, part):
    key = jax.random.fold_in(key, 5)
    key_base, key_rows, key_cols = jax.random.split(key, 3)
    base_draw = jax.random.truncated_normal(key_base, -4.0, 4.0, (TOKENS, D), jnp.float32)
    reach = 1.15
    row_scale = jnp.exp(jax.random.uniform(key_rows, (TOKENS, 1), jnp.float32, -reach, reach))
    col_scale = jnp.exp(jax.random.uniform(key_cols, (1, D), jnp.float32, -reach, reach))
    return (base_draw * row_scale * col_scale).astype(jnp.bfloat16)


def level_of(own_key, shape, pieces, low, top_value):
    factor_of, own = 1.0, jax.random.fold_in(own_key, 6)
    for dim, shards_of in pieces:
        draws = jnp.exp(jax.random.uniform(jax.random.fold_in(own, dim), (shards_of,), jnp.float32, low / len(pieces), top_value / len(pieces)))
        factor_of = factor_of * jnp.repeat(draws, shape[dim] // shards_of).reshape([-1 if axis == dim else 1 for axis in range(len(shape))])
    return factor_of


def shared_out(stream_key, own, number, rows, amount, top, most, lean):
    ranking = jax.random.permutation(stream_key, amount)
    packed, common = shares(amount, rows * top, most, lean, True), shares(amount, rows * top, most, lean, False)
    places = jnp.arange(amount)

    def named(sizes, rotation):
        used = int((sizes > 0).sum())
        fixed = max(1, used // 4)
        moved = fixed + (places - fixed + rotation * (used - fixed)) % max(1, amount - fixed)
        return jnp.zeros((amount,), jnp.int32).at[ranking[jnp.where(places < fixed, places, moved)]].set(jnp.asarray(sizes, jnp.int32))

    sizes = jnp.where(number % 4 == 0, named(packed, number // 4), named(common, number - number // 4 - 1))
    mixed = jax.random.permutation(jax.random.fold_in(own, 3), amount)
    source_of, sink = mixed[0:amount // 2 * 2:2], mixed[1:amount // 2 * 2:2]
    slack = jnp.minimum(sizes[source_of] - 1, most - sizes[sink]) // 2
    slack = jnp.where((source_of == ranking[0]) | (sink == ranking[0]) | (sizes[sink] == 0), 0, jnp.maximum(slack, 0))
    moved = jax.random.randint(jax.random.fold_in(own, 4), (amount // 2,), 0, 1 << 20) % (slack + 1)
    sizes = sizes.at[source_of].add(-moved).at[sink].add(moved)
    items = jnp.searchsorted(jnp.cumsum(sizes), jnp.arange(rows * top), side="right").astype(jnp.int32)
    listing = items.reshape(top, rows).T
    listing = listing[jax.random.permutation(jax.random.fold_in(own, 1), rows)]
    rotation = jax.random.randint(jax.random.fold_in(own, 2), (rows, 1), 0, top)
    return jnp.take_along_axis(listing, (jnp.arange(top)[None, :] + rotation) % top, axis=1)


def shares(amount, total, most, skew, full):
    portions = [(1 << 20) // math.isqrt(grade ** skew) + 1 for grade in range(1, amount + 1)]
    largest = most if full else min(most, max(-(-total // amount), total * portions[0] // sum(portions)))
    least = 1 if total - largest >= amount - 1 else 0
    given, rest = [largest] + [least] * (amount - 1), total - largest - least * (amount - 1)
    while rest > 0:
        movable = [i for i in range(1, amount) if given[i] < largest] or [i for i in range(1, amount) if given[i] < most]
        whole, budget = sum([portions[i] for i in movable]), rest
        for i in movable:
            addition = min(most - given[i], max(1, budget * portions[i] // whole), rest)
            given[i] = given[i] + addition
            rest = rest - addition
    return np.array(given)


def bell_draw(rng, dims, width, limit, cuts=(), kind=jnp.bfloat16):
    factor_of = level_of(rng, dims, cuts, -0.22, 0.18) if cuts else 1.0
    values = jax.random.normal(rng, dims, jnp.float32) * width * factor_of
    return jnp.minimum(jnp.maximum(values, -limit), limit).astype(kind)


def setup_inputs(seed: int = 0) -> dict:
    splits = jax.random.split(jax.random.key(seed), 10)
    context = bell_draw(splits[0], (TOKENS, D), 1.0, 6.0, ((0, 64),))
    residual = draw_residual(jax.random.fold_in(splits[9], 71), 0)
    branch_out_proj = bell_draw(splits[2], (EXPERTS, D, D), D ** -0.5, 0.09375, ((0, 4), (1, 16), (2, 4)))
    norm_gain = jnp.clip(1.0 + 0.15 * jax.random.normal(splits[3], (D,), jnp.float32), 0.25, 1.75).astype(jnp.bfloat16)
    router = bell_draw(splits[4], (D, EXPERTS), D ** -0.5, 0.09375)
    expert_ids_keys = jax.random.split(jax.random.fold_in(splits[5], 1), TOKENS // ROWS)
    expert_ids_turns = jax.random.permutation(jax.random.fold_in(splits[5], 3), TOKENS // ROWS)
    expert_ids = jax.vmap(lambda own, number: shared_out(jax.random.fold_in(splits[5], 2), own, number, ROWS, EXPERTS, 2, CAP, 2))(expert_ids_keys, expert_ids_turns).reshape((TOKENS, 2))
    gate_proj = bell_draw(splits[6], (EXPERTS, D, FF), D ** -0.5, 0.09375, ((0, 4), (2, 16)))
    up_proj = bell_draw(splits[7], (EXPERTS, D, FF), D ** -0.5, 0.09375, ((0, 4), (2, 16)))
    down_proj = bell_draw(splits[8], (EXPERTS, FF, D), FF ** -0.5, 0.078125, ((0, 4), (1, 16)))
    return dict(context=context, residual=residual, branch_out_proj=branch_out_proj, norm_gain=norm_gain, router=router, expert_ids=expert_ids, gate_proj=gate_proj, up_proj=up_proj, down_proj=down_proj)


def one_expert(operands):
    expert_in, gate_mat, up_mat, down_mat = operands
    gate_act = jnp.dot(expert_in, gate_mat, preferred_element_type=jnp.float32)
    up_act = jnp.dot(expert_in, up_mat, preferred_element_type=jnp.float32)
    hidden_act = (jax.nn.silu(gate_act) * up_act).astype(jnp.bfloat16)
    slot_rows = expert_in.shape[0]
    hidden_blocks = hidden_act.reshape(slot_rows, FF // FF_DEV, FF_DEV).transpose(1, 0, 2)
    down_blocks = down_mat.reshape(FF // FF_DEV, FF_DEV, D)

    def add_block(running_sum, block_pair):
        hidden_block, down_block = block_pair
        block_term = jnp.dot(hidden_block, down_block, preferred_element_type=jnp.float32).astype(jnp.bfloat16)
        block_term = lax.optimization_barrier(block_term)
        return (running_sum + block_term.astype(jnp.float32), None)
    running_sum, _ = lax.scan(add_block, jnp.zeros((slot_rows, D), jnp.float32), (hidden_blocks, down_blocks))
    return running_sum.astype(jnp.bfloat16)

def reference(context, residual, branch_out_proj, norm_gain, router, expert_ids, gate_proj, up_proj, down_proj):
    merged = lax.optimization_barrier(jnp.mean(branch_out_proj.astype(jnp.float32), axis=0)).astype(jnp.bfloat16)
    projected = jnp.dot(context, merged, preferred_element_type=jnp.float32)
    hidden_state = residual.astype(jnp.float32) + projected
    inv_rms = lax.rsqrt(lax.optimization_barrier(jnp.mean(hidden_state * hidden_state, axis=-1, keepdims=True)) + 1e-05)
    normed = (hidden_state * inv_rms * norm_gain.astype(jnp.float32)).astype(jnp.bfloat16)
    logits = jnp.dot(normed, router, preferred_element_type=jnp.float32)
    scores = jax.nn.sigmoid(logits)
    chosen = (expert_ids[:, :, None] == jnp.arange(EXPERTS, dtype=jnp.int32)[None, None, :]).astype(jnp.float32)
    selected = lax.optimization_barrier(jnp.sum(chosen * scores[:, None, :], axis=-1))
    gate_weights = selected / lax.optimization_barrier(jnp.sum(selected, axis=-1, keepdims=True))
    block_count = TOKENS // ROWS
    flat_ids = expert_ids.reshape(block_count, ROWS * 2)
    one_hot = (flat_ids[:, :, None] == jnp.arange(EXPERTS, dtype=jnp.int32)[None, None, :]).astype(jnp.int32)
    before = jnp.cumsum(one_hot, axis=1) - one_hot
    slot_index = lax.optimization_barrier(jnp.sum(before * one_hot, axis=-1)).astype(jnp.int32)
    target = flat_ids * CAP + slot_index
    dispatch = (target[:, :, None] == jnp.arange(EXPERTS * CAP, dtype=jnp.int32)[None, None, :]).astype(jnp.float32)
    dispatch = dispatch.reshape(block_count, ROWS, 2, EXPERTS * CAP)
    normed_blocks = normed.reshape(block_count, ROWS, D).astype(jnp.float32)
    buffer = jnp.einsum('ntkq,ntd->nqd', dispatch, normed_blocks).astype(jnp.bfloat16)
    expert_in = buffer.reshape(block_count, EXPERTS, CAP, D).transpose(1, 0, 2, 3).reshape(EXPERTS, block_count * CAP, D)
    results = lax.map(one_expert, (expert_in, gate_proj, up_proj, down_proj))
    returned = results.reshape(EXPERTS, block_count, CAP, D).transpose(1, 0, 2, 3).reshape(block_count, EXPERTS * CAP, D)
    picked = jnp.einsum('ntkq,nqd->ntkd', dispatch, returned.astype(jnp.float32)).reshape(TOKENS, 2, D)
    mixed = hidden_state + lax.optimization_barrier(jnp.sum(gate_weights[:, :, None] * picked, axis=1))
    return mixed.astype(jnp.bfloat16)
```

```python
import functools

import jax
import jax.numpy as jnp
from jax import lax
from jax.experimental import pallas as pl
from jax.experimental.pallas import tpu as pltpu
from jax.sharding import PartitionSpec as P

NX, NY, NZ = 4, 4, 8
MESH = pl.DeviceIdType.MESH
F32, BF16 = jnp.float32, jnp.bfloat16
GATES = 128


def position():
    b, d, x = lax.axis_index("branch"), lax.axis_index("dp"), lax.axis_index("mp")
    return x, (d % 2) * 2 + b // 2, d // 2, b % 2


def device(x, y, z, core):
    return {"branch": (y % 2) * 2 + core, "dp": z * 2 + y // 2, "mp": x}


def rows(start, size):
    return pl.ds(pl.multiple_of(start, size), size)


class Ring:
    def __init__(self, n, me, at, send, recv):
        self.n, self.me, self.at, self.send_sem, self.recv_sem = n, me, at, send, recv
        self.sent = []

    def near(self, step):
        return (self.me + step + self.n) % self.n

    def live(self, k, h, way):
        return k < self.n // 2 or h == way

    def lanes(self, k):
        return [(h, way) for h in (0, 1) for way in (0, 1) if self.live(k, h, way)]

    def copy(self, src, dst, k, h, way):
        return pltpu.make_async_remote_copy(
            src_ref=src,
            dst_ref=dst,
            send_sem=self.send_sem(way, k - 1, h),
            recv_sem=self.recv_sem(way, k - 1, h),
            device_id=self.at(self.near(1 if way == 0 else -1)),
            device_id_type=MESH,
        )

    def drain(self):
        for c in self.sent:
            c.wait_send()


class Gather(Ring):
    def __init__(self, n, me, at, send, recv, block):
        super().__init__(n, me, at, send, recv)
        self.block, self.seen = block, set()

    def start(self, k):
        for h, way in self.lanes(k):
            if k > 1:
                self.arrive(k - 1, h, way)
            part = self.block(self.near(1 - k if way == 0 else k - 1), h)
            c = self.copy(part, part, k, h, way)
            c.start()
            self.sent.append(c)

    def arrive(self, k, h, way):
        if (k, h, way) not in self.seen:
            self.seen.add((k, h, way))
            part = self.block(self.near(-k if way == 0 else k), h)
            self.copy(part, part, k, h, way).wait_recv()

    def arrived(self, k):
        for h, way in self.lanes(k):
            self.arrive(k, h, way)


class Scatter(Ring):
    def __init__(self, n, me, at, send, recv, block, landing):
        super().__init__(n, me, at, send, recv)
        self.block, self.landing = block, landing

    def live(self, k, h, way):
        return k > 1 or h == way

    def put(self, k, h, way):
        far = self.n // 2 - k + 1
        c = self.copy(
            self.block(self.near(far if way == 0 else -far), h), self.landing(way, k - 1, h), k, h, way
        )
        c.start()
        self.sent.append(c)

    def first(self):
        for h, way in self.lanes(1):
            self.put(1, h, way)
        for h in (0, 1):
            for way in (0, 1):
                if not self.live(1, h, way):
                    self.put(2, h, way)

    def advance(self, k):
        for h, way in self.lanes(k):
            arrived = self.landing(way, k - 1, h)
            self.copy(arrived, arrived, k, h, way).wait_recv()
            left = self.n // 2 - k
            mine = self.block(self.near(left if way == 0 else -left), h)
            mine[...] = (mine[...].astype(F32) + arrived[...].astype(F32)).astype(BF16)
            if left:
                self.put(k + 1, h, way)


def greet(peers):
    barrier = pltpu.get_barrier_semaphore()
    for peer in peers:
        pl.semaphore_signal(barrier, inc=1, device_id=peer, device_id_type=MESH)
    pl.semaphore_wait(barrier, len(peers))


def project_kernel(
    block_ref, context_ref, residual_ref, gain_ref, router_ref, ids_ref, gate_ref, up_ref, down_ref,
    token_ref, hidden_ref, gate_out, up_out, down_out,
    context_two, pieces, merged, total, part, parts,
    pair_send, pair_recv, ring_send, ring_recv, lane_send, lane_recv,
):
    x, y, z, core = position()
    other = 1 - core
    half = y % 2
    base = y - half
    mate = base + 1 - half
    peers = [device(x, y, z, other), device(x, mate, z, core), device(x, mate, z, other)]
    far_side = (y + 1 + 2 * (1 - half)) % NY
    peers += [device(x, far_side, z, core), device(x, y, (z + 1) % NZ, core), device(x, y, (z + 7) % NZ, core)]
    for dx in (1, 2, 3):
        for c in (core, other):
            peers.append(device((x + dx) % NX, y, z, c))
    greet(peers)

    def pair_copy(i, src, dst, to):
        return pltpu.make_async_remote_copy(
            src_ref=src, dst_ref=dst, send_sem=pair_send.at[i], recv_sem=pair_recv.at[i],
            device_id=to, device_id_type=MESH,
        )

    tall, wide = block_ref.shape[0] // 2, block_ref.shape[1] // 2
    pending = []
    for i, (dy, dc) in enumerate(((0, 1), (1, 0), (1, 1))):
        to_half = half if dy == 0 else 1 - half
        to_core = core if dc == 0 else other
        pending.append(pair_copy(
            i, block_ref.at[rows(to_half * tall, tall), rows(to_core * wide, wide)], pieces.at[i],
            device(x, base + to_half, z, to_core),
        ))
    sibling = device(x, y, z, other)
    pending.append(pair_copy(3, context_ref, context_two, sibling))
    pending.append(pair_copy(4, gate_ref, gate_out, sibling))
    pending.append(pair_copy(5, up_ref, up_out, sibling))
    pending.append(pair_copy(6, down_ref, down_out, sibling))
    for c in pending:
        c.start()
    for c in pending[:3]:
        c.wait_recv()
    own = block_ref[rows(half * tall, tall), rows(core * wide, wide)].astype(F32)
    own = own + pieces[0].astype(F32) + pieces[1].astype(F32) + pieces[2].astype(F32)
    merged[z, rows(y * tall, tall), :] = (own * 0.25).astype(BF16)

    quarter = wide // 2

    def ring_sems(i):
        return (lambda way, k, h: ring_send.at[i, way, k, h]), (lambda way, k, h: ring_recv.at[i, way, k, h])

    at_y = lambda p: device(x, p, z, core)
    at_z = lambda p: device(x, y, p, core)
    a_y = Gather(NY, y, at_y, *ring_sems(0), lambda i, h: merged.at[
        z, rows(i * tall + h * (tall // 2), tall // 2), pl.ds(0, quarter)])
    b_z = Gather(NZ, z, at_z, *ring_sems(1), lambda i, h: merged.at[
        i, rows(y * tall + h * (tall // 2), tall // 2), pl.ds(quarter, quarter)])
    a_z = Gather(NZ, z, at_z, *ring_sems(2), lambda i, h: merged.at[
        i, pl.ds(h * 2 * tall, 2 * tall), pl.ds(0, quarter)])
    b_y = Gather(NY, y, at_y, *ring_sems(3), lambda i, h: merged.at[
        pl.ds(h * 4, 4), rows(i * tall, tall), pl.ds(quarter, quarter)])
    gather_all(a_y, b_z, a_z, b_y, {})

    pending[3].wait_recv()
    total[...] = jnp.zeros_like(total)

    @pl.loop(0, NZ)
    def _(k):
        depth = rows(k * 4 * tall, 4 * tall)
        total[0] += jnp.dot(context_ref[:, depth], merged[k], preferred_element_type=F32)
        total[1] += jnp.dot(context_two[:, depth], merged[k], preferred_element_type=F32)

    part[...] = total[...].astype(BF16)
    few = residual_ref.shape[0] // NX
    parts[x * 2 + core] = part[0, rows(x * few, few), :]
    lanes = []
    for dx in range(NX):
        for dc in range(2):
            if dx or dc:
                to_x = (x + dx) % NX
                c = pltpu.make_async_remote_copy(
                    src_ref=part.at[dc, rows(to_x * few, few), :],
                    dst_ref=parts.at[x * 2 + core],
                    send_sem=lane_send.at[dx * 2 + dc], recv_sem=lane_recv.at[dx * 2 + dc],
                    device_id=device(to_x, y, z, core if dc == 0 else other), device_id_type=MESH,
                )
                c.start()
                lanes.append((dx, dc, c))
    for dx, dc, c in lanes:
        land = parts.at[(x + NX - dx) % NX * 2 + (core if dc == 0 else other)]
        pltpu.make_async_remote_copy(
            src_ref=land, dst_ref=land,
            send_sem=lane_send.at[dx * 2 + dc], recv_sem=lane_recv.at[dx * 2 + dc],
            device_id=sibling, device_id_type=MESH,
        ).wait_recv()
    here = rows(x * few, few)
    features = residual_ref.shape[1]
    squares = jnp.zeros((few, 1), F32)
    for j in range(2 * NX):
        columns = pl.ds(j * wide, wide)
        hidden = residual_ref[here, columns].astype(F32) + parts[j].astype(F32)
        hidden_ref[:, columns] = hidden
        squares = squares + jnp.sum(hidden * hidden, axis=-1, keepdims=True)
    inv_rms = lax.rsqrt(squares / features + 1e-05)
    logits = jnp.zeros((few, GATES), F32)
    for j in range(2 * NX):
        columns = pl.ds(j * wide, wide)
        normed = (hidden_ref[:, columns] * inv_rms * gain_ref[:, columns].astype(F32)).astype(BF16)
        token_ref[:, columns] = normed
        logits = logits + jnp.dot(normed, router_ref[columns, :], preferred_element_type=F32)
    scores = 1.0 / (1.0 + jnp.exp(-logits))
    lane = lax.broadcasted_iota(jnp.int32, (few, GATES), 1)
    expert = lane % 4
    ids = ids_ref[here, :]
    first, second = ids[:, 0:1] == expert, ids[:, 1:2] == expert
    once = lane < 4
    picked_first = jnp.sum(jnp.where(first & once, scores, 0.0), axis=-1, keepdims=True)
    picked_second = jnp.sum(jnp.where(second & once, scores, 0.0), axis=-1, keepdims=True)
    weight = jnp.where(first, picked_first, jnp.where(second, picked_second, 0.0))
    weight = weight / (picked_first + picked_second)
    high = weight.astype(BF16).astype(F32)
    mid = (weight - high).astype(BF16).astype(F32)
    low = weight - high - mid
    sent = jnp.where(lane < 4, high, jnp.where(lane < 8, mid, jnp.where(lane < 12, low, 0.0)))
    token_ref[:, pl.ds(features, GATES)] = sent.astype(BF16)

    for c in pending[4:]:
        c.wait_recv()
    for c in pending:
        c.wait_send()
    for ring in (a_y, b_z, a_z, b_y):
        ring.drain()
    for _, _, c in lanes:
        c.wait_send()


def gather_all(a_y, b_z, a_z, b_y, then):
    run = lambda name: then.get(name, lambda: None)()
    a_y.start(1)
    b_z.start(1)
    a_y.start(2)
    b_z.start(2)
    a_y.arrived(1)
    a_y.arrived(2)
    a_z.start(1)
    b_z.start(3)
    b_z.start(4)
    for k in (1, 2, 3, 4):
        b_z.arrived(k)
    b_y.start(1)
    run("a0")
    a_z.start(2)
    run("b0")
    a_z.arrived(1)
    run("a1")
    a_z.start(3)
    b_y.start(2)
    a_z.arrived(2)
    run("a2")
    a_z.start(4)
    b_y.arrived(1)
    run("b1")
    a_z.arrived(3)
    run("a3")
    b_y.arrived(2)
    run("b2")
    a_z.arrived(4)
    run("a4")


def expert_kernel(
    token_ref, hidden_ref, gate_own, up_own, down_own, gate_two, up_two, down_two,
    out_ref,
    tok_a, tok_b, enter, leave, act, inner, sum_a, sum_b, land_az, land_by, land_ay, land_bz, mixed,
    load_sem, ring_send, ring_recv, lane_send, lane_recv,
):
    x, y, z, core = position()
    peers = [device(x, (y + 1) % NY, z, core), device(x, (y + 3) % NY, z, core)]
    peers += [device(x, y, (z + 1) % NZ, core), device(x, y, (z + 7) % NZ, core)]
    peers += [device((x + dx) % NX, y, z, core) for dx in (1, 2, 3)]
    width = gate_own.shape[1]
    loads = []
    for i, (src, dst) in enumerate((
        (gate_own, enter.at[:, pl.ds(0, width)]),
        (up_own, enter.at[:, pl.ds(width, width)]),
        (gate_two, enter.at[:, pl.ds(2 * width, width)]),
        (up_two, enter.at[:, pl.ds(3 * width, width)]),
        (down_own, leave.at[pl.ds(0, width), :]),
        (down_two, leave.at[pl.ds(width, width), :]),
    )):
        c = pltpu.make_async_copy(src, dst, load_sem.at[i])
        c.start()
        loads.append(c)
    features = hidden_ref.shape[1]
    tall = token_ref.shape[0] // 2
    tok_a[z, rows(y * tall, tall), :] = token_ref[pl.ds(0, tall), :]
    tok_b[y, rows(z * tall, tall), :] = token_ref[pl.ds(tall, tall), :]
    greet(peers)

    def ring_sems(i):
        return (lambda way, k, h: ring_send.at[i, way, k, h]), (lambda way, k, h: ring_recv.at[i, way, k, h])

    at_y = lambda p: device(x, p, z, core)
    at_z = lambda p: device(x, y, p, core)
    cut = features // 2

    def wide_part(h):
        return pl.ds(0, cut) if h == 0 else pl.ds(cut, cut + GATES)

    a_y = Gather(NY, y, at_y, *ring_sems(0), lambda i, h: tok_a.at[z, rows(i * tall, tall), wide_part(h)])
    b_z = Gather(NZ, z, at_z, *ring_sems(1), lambda i, h: tok_b.at[y, rows(i * tall, tall), wide_part(h)])
    a_z = Gather(NZ, z, at_z, *ring_sems(2), lambda i, h: tok_a.at[i, pl.ds(h * 2 * tall, 2 * tall), :])
    b_y = Gather(NY, y, at_y, *ring_sems(3), lambda i, h: tok_b.at[i, pl.ds(h * 4 * tall, 4 * tall), :])

    own_expert = (y % 2) * 2 + core
    two_expert = (y % 2) * 2 + 1 - core
    tile = 256

    def experts(tok, block, out):
        size = tok.shape[1]

        @pl.loop(0, enter.shape[1] // tile)
        def _(n):
            columns = rows(n * tile, tile)
            act[pl.ds(0, size), columns] = jnp.dot(
                tok[block, :, pl.ds(0, features)], enter[:, columns], preferred_element_type=F32
            )

        sent = tok[block, :, pl.ds(features, GATES)].astype(F32)
        expert = lax.broadcasted_iota(jnp.int32, sent.shape, 1) % 4
        for s, e in ((0, own_expert), (1, two_expert)):
            weight = jnp.sum(jnp.where(expert == e, sent, 0.0), axis=-1, keepdims=True)
            g = act[pl.ds(0, size), pl.ds(2 * s * width, width)]
            u = act[pl.ds(0, size), pl.ds((2 * s + 1) * width, width)]
            inner[pl.ds(0, size), pl.ds(s * width, width)] = (g / (1.0 + jnp.exp(-g)) * u * weight).astype(BF16)

        @pl.loop(0, features // tile)
        def _(n):
            columns = rows(n * tile, tile)
            out[block, :, columns] = jnp.dot(
                inner[pl.ds(0, size), :], leave[:, columns], preferred_element_type=F32
            ).astype(BF16)

    def do_a(k):
        def body(i, carry):
            experts(tok_a, (z + k * (1 - 2 * i) + NZ) % NZ, sum_a)
            return carry

        def go():
            if k == 0:
                for c in loads:
                    c.wait()
            lax.fori_loop(0, 1 if k in (0, 4) else 2, body, 0)
        return go

    def do_b(k):
        def body(i, carry):
            experts(tok_b, (y + k * (1 - 2 * i) + NY) % NY, sum_b)
            return carry

        return lambda: lax.fori_loop(0, 1 if k in (0, 2) else 2, body, 0)

    gather_all(a_y, b_z, a_z, b_y, {
        "a0": do_a(0), "a1": do_a(1), "a2": do_a(2), "a3": do_a(3), "a4": do_a(4),
        "b0": do_b(0), "b1": do_b(1), "b2": do_b(2),
    })

    def narrow_part(h):
        return pl.ds(h * cut, cut)

    s_az = Scatter(NZ, z, at_z, *ring_sems(4), lambda i, h: sum_a.at[i, pl.ds(h * 2 * tall, 2 * tall), :],
                   lambda way, k, h: land_az.at[way, k, pl.ds(h * 2 * tall, 2 * tall), :])
    s_by = Scatter(NY, y, at_y, *ring_sems(5), lambda i, h: sum_b.at[i, pl.ds(h * 4 * tall, 4 * tall), :],
                   lambda way, k, h: land_by.at[way, k, pl.ds(h * 4 * tall, 4 * tall), :])
    s_ay = Scatter(NY, y, at_y, *ring_sems(6), lambda i, h: sum_a.at[z, rows(i * tall, tall), narrow_part(h)],
                   lambda way, k, h: land_ay.at[way, k, :, narrow_part(h)])
    s_bz = Scatter(NZ, z, at_z, *ring_sems(7), lambda i, h: sum_b.at[y, rows(i * tall, tall), narrow_part(h)],
                   lambda way, k, h: land_bz.at[way, k, :, narrow_part(h)])
    s_by.first()
    s_az.first()
    s_az.advance(1)
    s_by.advance(1)
    s_az.advance(2)
    s_az.advance(3)
    s_by.advance(2)
    s_bz.first()
    s_az.advance(4)
    s_ay.first()
    s_bz.advance(1)
    s_ay.advance(1)
    s_bz.advance(2)
    s_ay.advance(2)
    s_bz.advance(3)
    s_bz.advance(4)

    low, high = pl.ds(0, tall), pl.ds(tall, tall)
    mixed[x, low, :] = (hidden_ref[low, :] + sum_a[z, rows(y * tall, tall), :].astype(F32)).astype(BF16)
    mixed[x, high, :] = (hidden_ref[high, :] + sum_b[y, rows(z * tall, tall), :].astype(F32)).astype(BF16)
    lanes = []
    for dx in (1, 2, 3):
        c = pltpu.make_async_remote_copy(
            src_ref=mixed.at[x], dst_ref=mixed.at[x],
            send_sem=lane_send.at[dx], recv_sem=lane_recv.at[dx],
            device_id=device((x + dx) % NX, y, z, core), device_id_type=MESH,
        )
        c.start()
        lanes.append(c)
    few = 2 * tall
    out_ref[rows(x * few, few), :] = mixed[x]
    for dx in (1, 2, 3):
        source = (x + NX - dx) % NX
        land = mixed.at[source]
        pltpu.make_async_remote_copy(
            src_ref=land, dst_ref=land,
            send_sem=lane_send.at[dx], recv_sem=lane_recv.at[dx],
            device_id=device(source, y, z, core), device_id_type=MESH,
        ).wait_recv()
        out_ref[rows(source * few, few), :] = mixed[source]
    for ring in (a_y, b_z, a_z, b_y, s_az, s_by, s_ay, s_bz):
        ring.drain()
    for c in lanes:
        c.wait_send()


def local(
    context, residual, branch_out_proj, norm_gain, router, expert_ids, gate_proj, up_proj, down_proj
):
    token_count, features = residual.shape
    few = token_count // NX
    half = few // 2
    width = gate_proj.shape[2]
    tall, wide = branch_out_proj.shape[1] // 2, branch_out_proj.shape[2] // 2
    vmem, hbm = pl.BlockSpec(memory_space=pltpu.VMEM), pl.BlockSpec(memory_space=pl.ANY)
    dma = pltpu.SemaphoreType.DMA
    router_lanes = jnp.pad(jnp.concatenate([router] * 3, axis=1), ((0, 0), (0, GATES - 12)))
    gate, up, down = gate_proj[0], up_proj[0], down_proj[0]
    shaped = jax.ShapeDtypeStruct
    tokens, hidden, gate_two, up_two, down_two = pl.pallas_call(
        project_kernel,
        out_shape=(
            shaped((few, features + GATES), BF16), shaped((few, features), F32),
            shaped(gate.shape, BF16), shaped(up.shape, BF16), shaped(down.shape, BF16),
        ),
        in_specs=[vmem] * 6 + [hbm] * 3,
        out_specs=(vmem, vmem, hbm, hbm, hbm),
        scratch_shapes=[
            pltpu.VMEM((token_count, features), BF16),
            pltpu.VMEM((3, tall, wide), BF16),
            pltpu.VMEM((NZ, NY * tall, wide), BF16),
            pltpu.VMEM((2, token_count, wide), F32),
            pltpu.VMEM((2, token_count, wide), BF16),
            pltpu.VMEM((2 * NX, few, wide), BF16),
            dma((7,)), dma((7,)), dma((4, 2, 4, 2)), dma((4, 2, 4, 2)), dma((8,)), dma((8,)),
        ],
        compiler_params=pltpu.CompilerParams(
            collective_id=0, has_side_effects=True, vmem_limit_bytes=40 * 2**20
        ),
        name="merge_and_project",
    )(branch_out_proj[0], context, residual, norm_gain.reshape(1, features), router_lanes, expert_ids, gate, up, down)
    return pl.pallas_call(
        expert_kernel,
        out_shape=shaped((token_count, features), BF16),
        in_specs=[vmem] * 2 + [hbm] * 6,
        out_specs=vmem,
        scratch_shapes=[
            pltpu.VMEM((NZ, NY * half, features + GATES), BF16),
            pltpu.VMEM((NY, NZ * half, features + GATES), BF16),
            pltpu.VMEM((features, 4 * width), BF16),
            pltpu.VMEM((2 * width, features), BF16),
            pltpu.VMEM((NZ * half, 4 * width), F32),
            pltpu.VMEM((NZ * half, 2 * width), BF16),
            pltpu.VMEM((NZ, NY * half, features), BF16),
            pltpu.VMEM((NY, NZ * half, features), BF16),
            pltpu.VMEM((2, 4, NY * half, features), BF16),
            pltpu.VMEM((2, 2, NZ * half, features), BF16),
            pltpu.VMEM((2, 2, half, features), BF16),
            pltpu.VMEM((2, 4, half, features), BF16),
            pltpu.VMEM((NX, few, features), BF16),
            dma((6,)), dma((8, 2, 4, 2)), dma((8, 2, 4, 2)), dma((4,)), dma((4,)),
        ],
        compiler_params=pltpu.CompilerParams(
            collective_id=1, has_side_effects=True, vmem_limit_bytes=60 * 2**20
        ),
        name="experts",
    )(tokens, hidden, gate, up, down, gate_two, up_two, down_two)


def solution(mesh):
    placed = (
        P(("branch", "dp"), None),
        P(("branch", "dp"), None),
        P("branch", "dp", "mp"),
        P(),
        P(),
        P(("branch", "dp"), None),
        P("branch", None, "dp"),
        P("branch", None, "dp"),
        P("branch", "dp", None),
    )
    return jax.shard_map(
        local, mesh=mesh, in_specs=placed, out_specs=P(("branch", "dp"), None), check_vma=False
    )
```

```python
import jax
import jax.numpy as jnp
from jax import lax
from jax.experimental import pallas as pl
from jax.experimental.pallas import tpu as pltpu
from jax.sharding import PartitionSpec as P

NX, NY, NZ = 4, 4, 8
MESH = pl.DeviceIdType.MESH
F32, BF16 = jnp.float32, jnp.bfloat16
GATES = 128
FIRST, SECOND = 0, 1


def position():
    b, d, x = lax.axis_index("branch"), lax.axis_index("dp"), lax.axis_index("mp")
    return x, (d % 2) * 2 + b // 2, d // 2, b % 2


def device(x, y, z, core):
    return {"branch": (y % 2) * 2 + core, "dp": z * 2 + y // 2, "mp": x}


def rows(start, size):
    return pl.ds(pl.multiple_of(start, size), size)


class Ring:
    def __init__(self, n, me, at, send, recv):
        self.n, self.me, self.at, self.send_sem, self.recv_sem = n, me, at, send, recv
        self.sent = []

    def near(self, step):
        return (self.me + step + self.n) % self.n

    def copy(self, src, dst, k, h, way):
        return pltpu.make_async_remote_copy(
            src_ref=src,
            dst_ref=dst,
            send_sem=self.send_sem(way, k - 1, h),
            recv_sem=self.recv_sem(way, k - 1, h),
            device_id=self.at(self.near(1 if way == 0 else -1)),
            device_id_type=MESH,
        )

    def launch(self, src, dst, k, h, way):
        c = self.copy(src, dst, k, h, way)
        c.start()
        self.sent.append(c)

    def drain(self):
        for c in self.sent:
            c.wait_send()


class Gather(Ring):
    def __init__(self, n, me, at, send, recv, block, sliding=False):
        super().__init__(n, me, at, send, recv)
        self.block, self.sliding, self.seen = block, sliding, set()

    def lanes(self, k, turn):
        if turn == SECOND and k == self.n // 2:
            return []
        return [(way if turn == FIRST else 1 - way, way) for way in (0, 1)]

    def hop(self, k, h, way):
        if k > 1:
            self.arrive(k - 1, h, way)
        sign = -1 if way == 0 else 1
        src = self.block(sign * (k - 1), h)
        self.launch(src, self.block(sign * k, h) if self.sliding else src, k, h, way)

    def start(self, k, turn=None):
        for t in (FIRST, SECOND) if turn is None else (turn,):
            for h, way in self.lanes(k, t):
                self.hop(k, h, way)

    def arrive(self, k, h, way):
        if (k, h, way) not in self.seen:
            self.seen.add((k, h, way))
            part = self.block(-k if way == 0 else k, h)
            self.copy(part, part, k, h, way).wait_recv()

    def arrived(self, k):
        for t in (FIRST, SECOND):
            for h, way in self.lanes(k, t):
                self.arrive(k, h, way)


class Scatter(Ring):
    def __init__(self, n, me, at, send, recv, block, landing):
        super().__init__(n, me, at, send, recv)
        self.block, self.landing = block, landing

    def put(self, k, h, way):
        far = self.n // 2 - k + 1
        self.launch(self.block(far if way == 0 else -far, h), self.landing(way, k - 1, h), k, h, way)

    def first(self):
        for way in (0, 1):
            self.put(1, way, way)
        for way in (0, 1):
            self.put(2, 1 - way, way)

    def advance(self, k, turn=None):
        for t in (FIRST, SECOND) if turn is None else (turn,):
            if k == 1 and t == FIRST:
                continue
            for way in (0, 1):
                h = 1 - way if t == FIRST else way
                arrived = self.landing(way, k - 1, h)
                self.copy(arrived, arrived, k, h, way).wait_recv()
                left = self.n // 2 - k
                mine = self.block(left if way == 0 else -left, h)
                mine[...] = (mine[...].astype(F32) + arrived[...].astype(F32)).astype(BF16)
                if left:
                    self.put(k + 1, h, way)


def greet(peers):
    barrier = pltpu.get_barrier_semaphore()
    for peer in peers:
        pl.semaphore_signal(barrier, inc=1, device_id=peer, device_id_type=MESH)
    pl.semaphore_wait(barrier, len(peers))


A_ROWS = {0: 0, -1: 192, 1: 256, -2: 320, 2: 384, -3: 704, 3: 768, 4: 832, -4: 832}
B_ROWS = {0: 64, -1: 448, 1: 576, 2: 896, -2: 896}


def layer_kernel(
    block_ref, context_ref, residual_ref, gain_ref, router_ref, ids_ref, gate_ref, up_ref, down_ref,
    out_ref,
    context_all, pieces, merged, total, part, parts, hidden_ref,
    tok, enter, leave, act, inner, sums, land_az, land_by, land_ay, land_bz, mixed,
    load_sem, pair_send, pair_recv, ring_send, ring_recv, lane_send, lane_recv,
):
    x, y, z, core = position()
    other = 1 - core
    half = y % 2
    base = y - half
    mate = base + 1 - half
    width = gate_ref.shape[1]
    tokens, features = context_ref.shape
    loads = []
    for i, (src, dst) in enumerate((
        (context_ref, context_all.at[pl.ds(0, tokens), :]),
        (gate_ref, enter.at[:, pl.ds(0, width)]),
        (up_ref, enter.at[:, pl.ds(width, width)]),
        (down_ref, leave.at[pl.ds(0, width), :]),
    )):
        c = pltpu.make_async_copy(src, dst, load_sem.at[i])
        c.start()
        loads.append(c)
    peers = [device(x, y, z, other), device(x, mate, z, core), device(x, mate, z, other)]
    far_side = (y + 1 + 2 * (1 - half)) % NY
    peers += [device(x, far_side, z, core), device(x, y, (z + 1) % NZ, core), device(x, y, (z + 7) % NZ, core)]
    for dx in (1, 2, 3):
        for c in (core, other):
            peers.append(device((x + dx) % NX, y, z, c))
    greet(peers)

    def pair_copy(i, src, dst, to):
        return pltpu.make_async_remote_copy(
            src_ref=src, dst_ref=dst, send_sem=pair_send.at[i], recv_sem=pair_recv.at[i],
            device_id=to, device_id_type=MESH,
        )

    tall, wide = block_ref.shape[0] // 2, block_ref.shape[1] // 2
    sibling = device(x, y, z, other)
    pending = []
    for i, (dy, dc) in enumerate(((0, 1), (1, 0), (1, 1))):
        to_half = half if dy == 0 else 1 - half
        to_core = core if dc == 0 else other
        pending.append(pair_copy(
            i, block_ref.at[rows(to_half * tall, tall), rows(to_core * wide, wide)], pieces.at[i],
            device(x, base + to_half, z, to_core),
        ))
    pending.append(pair_copy(3, context_ref, context_all.at[pl.ds(tokens, tokens), :], sibling))
    pending.append(pair_copy(4, gate_ref, enter.at[:, pl.ds(2 * width, width)], sibling))
    pending.append(pair_copy(5, up_ref, enter.at[:, pl.ds(3 * width, width)], sibling))
    pending.append(pair_copy(6, down_ref, leave.at[pl.ds(width, width), :], sibling))
    for c in pending:
        c.start()
    for c in pending[:3]:
        c.wait_recv()
    own = block_ref[rows(half * tall, tall), rows(core * wide, wide)].astype(F32)
    own = own + pieces[0].astype(F32) + pieces[1].astype(F32) + pieces[2].astype(F32)
    merged[z, rows(y * tall, tall), :] = (own * 0.25).astype(BF16)

    quarter = wide // 2

    def ring_sems(i):
        return (lambda way, k, h: ring_send.at[i, way, k, h]), (lambda way, k, h: ring_recv.at[i, way, k, h])

    at_y = lambda p: device(x, p, z, core)
    at_z = lambda p: device(x, y, p, core)
    near_y = lambda r: (y + r + NY) % NY
    near_z = lambda r: (z + r + NZ) % NZ
    piece = tall // 2
    a_y = Gather(NY, y, at_y, *ring_sems(0), lambda r, h: merged.at[
        z, rows(near_y(r) * tall + h * piece, piece), pl.ds(0, quarter)])
    b_z = Gather(NZ, z, at_z, *ring_sems(1), lambda r, h: merged.at[
        near_z(r), rows(y * tall + h * piece, piece), pl.ds(quarter, quarter)])
    a_z = Gather(NZ, z, at_z, *ring_sems(2), lambda r, h: merged.at[
        near_z(r), pl.ds(h * 2 * tall, 2 * tall), pl.ds(0, quarter)])
    b_y = Gather(NY, y, at_y, *ring_sems(3), lambda r, h: merged.at[
        pl.ds(h * 4, 4), rows(near_y(r) * tall, tall), pl.ds(quarter, quarter)])
    rings = [a_y, b_z, a_z, b_y]

    left, right = pl.ds(0, quarter), pl.ds(quarter, quarter)

    def project_a(*distances):
        for r in distances:
            i = near_z(r)
            term = jnp.dot(
                context_all[:, rows(i * 4 * tall, 4 * tall)], merged[i, :, left], preferred_element_type=F32
            )
            total[:, left] = term if r == 0 else total[:, left] + term

    def project_b(*distances):
        for r in distances:
            i = near_y(r)
            term = None
            for k in range(NZ):
                one = jnp.dot(
                    context_all[:, rows(i * tall + k * 4 * tall, tall)], merged[k, rows(i * tall, tall), right],
                    preferred_element_type=F32,
                )
                term = one if term is None else term + one
            total[:, right] = term if r == 0 else total[:, right] + term

    short_phase(a_y, b_z, a_z, b_y)
    loads[0].wait()
    pending[3].wait_recv()
    project_a(0)
    a_z.start(2, FIRST)
    project_b(0)
    a_z.start(2, SECOND)
    project_a(-1, 1)
    b_y.start(2)
    a_z.start(3, FIRST)
    a_z.start(3, SECOND)
    project_a(-2, 2)
    b_y.arrived(1)
    a_z.start(4)
    project_b(-1, 1)
    a_z.arrived(3)
    project_a(-3, 3)
    b_y.arrived(2)
    project_b(2)
    a_z.arrived(4)
    project_a(4)

    part[...] = total[...].astype(BF16)
    few = tokens // NX
    parts[x * 2 + core] = part[rows(x * few, few), :]
    lanes = []
    for dx in (2, 1, 3, 0):
        for dc in range(2):
            if dx or dc:
                to_x = (x + dx) % NX
                c = pltpu.make_async_remote_copy(
                    src_ref=part.at[rows(to_x * few + dc * tokens, few), :],
                    dst_ref=parts.at[x * 2 + core],
                    send_sem=lane_send.at[dx * 2 + dc], recv_sem=lane_recv.at[dx * 2 + dc],
                    device_id=device(to_x, y, z, core if dc == 0 else other), device_id_type=MESH,
                )
                c.start()
                lanes.append((dx, dc, c))
    for dx, dc, c in lanes:
        land = parts.at[(x + NX - dx) % NX * 2 + (core if dc == 0 else other)]
        pltpu.make_async_remote_copy(
            src_ref=land, dst_ref=land,
            send_sem=lane_send.at[dx * 2 + dc], recv_sem=lane_recv.at[dx * 2 + dc],
            device_id=sibling, device_id_type=MESH,
        ).wait_recv()
    here = rows(x * few, few)
    squares = jnp.zeros((few, 1), F32)
    for j in range(2 * NX):
        columns = pl.ds(j * wide, wide)
        hidden = residual_ref[here, columns].astype(F32) + parts[j].astype(F32)
        hidden_ref[:, columns] = hidden
        squares = squares + jnp.sum(hidden * hidden, axis=-1, keepdims=True)
    inv_rms = lax.rsqrt(squares / features + 1e-05)
    short = few // 2
    slot_a = rows(A_ROWS[0] + y * short, short)
    slot_b = rows(B_ROWS[0] + z * short, short)
    logits = jnp.zeros((few, 4), F32)
    for j in range(2 * NX):
        columns = pl.ds(j * wide, wide)
        normed = (hidden_ref[:, columns] * inv_rms * gain_ref[:, columns].astype(F32)).astype(BF16)
        tok[slot_a, columns] = normed[:short]
        tok[slot_b, columns] = normed[short:]
        logits = logits + lax.dot_general(
            normed, router_ref[:, columns], (((1,), (1,)), ((), ())), preferred_element_type=F32
        )
    lane = lax.broadcasted_iota(jnp.int32, (few, GATES), 1)
    row = lax.broadcasted_iota(jnp.int32, (few, GATES), 0)
    expert = lane % 4
    scores = 1.0 / (1.0 + jnp.exp(-logits))
    score_lanes = jnp.zeros((few, GATES), F32)
    for e in range(4):
        score_lanes = jnp.where(expert == e, scores[:, e:e + 1], score_lanes)
    ids = ids_ref[...].astype(F32)
    mine = lane == row + x * few
    first, second = (
        jnp.sum(jnp.where(mine, ids[k:k + 1, :], 0.0), axis=-1, keepdims=True) == expert.astype(F32) for k in (0, 1)
    )
    once = lane < 4
    picked_first = jnp.sum(jnp.where(first & once, score_lanes, 0.0), axis=-1, keepdims=True)
    picked_second = jnp.sum(jnp.where(second & once, score_lanes, 0.0), axis=-1, keepdims=True)
    weight = jnp.where(first, picked_first, jnp.where(second, picked_second, 0.0))
    weight = weight / (picked_first + picked_second)
    high = weight.astype(BF16).astype(F32)
    mid = (weight - high).astype(BF16).astype(F32)
    low = weight - high - mid
    sent = jnp.where(lane < 4, high, jnp.where(lane < 8, mid, jnp.where(lane < 12, low, 0.0))).astype(BF16)
    tok[slot_a, pl.ds(features, GATES)] = sent[:short]
    tok[slot_b, pl.ds(features, GATES)] = sent[short:]

    cut = features // 2

    def token_part(h):
        return pl.ds(0, cut) if h == 0 else pl.ds(cut, cut + GATES)

    def sum_part(h):
        return pl.ds(h * cut, cut)

    in_a = lambda p: rows(A_ROWS[0] + p * short, short)
    in_b = lambda p: rows(B_ROWS[0] + p * short, short)
    part_a = lambda r, h: pl.ds(A_ROWS[r] + h * 2 * short, 2 * short)
    part_b = lambda r, h: pl.ds(B_ROWS[r] + h * 4 * short, 4 * short)
    a_y = Gather(NY, y, at_y, *ring_sems(4), lambda r, h: tok.at[in_a(near_y(r)), token_part(h)])
    b_z = Gather(NZ, z, at_z, *ring_sems(5), lambda r, h: tok.at[in_b(near_z(r)), token_part(h)])
    a_z = Gather(NZ, z, at_z, *ring_sems(6), lambda r, h: tok.at[part_a(r, h), :], True)
    b_y = Gather(NY, y, at_y, *ring_sems(7), lambda r, h: tok.at[part_b(r, h), :], True)
    s_az = Scatter(NZ, z, at_z, *ring_sems(8), lambda r, h: sums.at[part_a(r, h), :],
                   lambda way, k, h: land_az.at[way, k, pl.ds(h * 2 * short, 2 * short), :])
    s_by = Scatter(NY, y, at_y, *ring_sems(9), lambda r, h: sums.at[part_b(r, h), :],
                   lambda way, k, h: land_by.at[way, k, pl.ds(h * 4 * short, 4 * short), :])
    s_ay = Scatter(NY, y, at_y, *ring_sems(10), lambda r, h: sums.at[in_a(near_y(r)), sum_part(h)],
                   lambda way, k, h: land_ay.at[way, k, :, sum_part(h)])
    s_bz = Scatter(NZ, z, at_z, *ring_sems(11), lambda r, h: sums.at[in_b(near_z(r)), sum_part(h)],
                   lambda way, k, h: land_bz.at[way, k, :, sum_part(h)])
    rings += [a_y, b_z, a_z, b_y, s_az, s_by, s_ay, s_bz]

    own_expert = half * 2 + core
    two_expert = half * 2 + other

    def expand(start, size):
        span, top = pl.ds(start, size), pl.ds(0, size)
        tile = 2 * width

        @pl.loop(0, 2)
        def _(n):
            columns = rows(n * tile, tile)
            act[top, columns] = jnp.dot(
                tok[span, pl.ds(0, features)], enter[:, columns], preferred_element_type=F32
            )

        gates = tok[span, pl.ds(features, GATES)].astype(F32)
        names = lax.broadcasted_iota(jnp.int32, gates.shape, 1) % 4
        for s, e in ((0, own_expert), (1, two_expert)):
            scale = jnp.sum(jnp.where(names == e, gates, 0.0), axis=-1, keepdims=True)
            g = act[top, pl.ds(2 * s * width, width)]
            u = act[top, pl.ds((2 * s + 1) * width, width)]
            inner[span, pl.ds(s * width, width)] = (g / (1.0 + jnp.exp(-g)) * u * scale).astype(BF16)

    def contract(start, size):
        span = pl.ds(start, size)
        tile = features // 2

        @pl.loop(0, 2)
        def _(n):
            columns = rows(n * tile, tile)
            sums[span, columns] = jnp.dot(
                inner[span, :], leave[:, columns], preferred_element_type=F32
            ).astype(BF16)

    short_phase(a_y, b_z, a_z, b_y)
    for c in loads[1:]:
        c.wait()
    for c in pending[4:]:
        c.wait_recv()
    expand(0, 192)
    a_z.start(2, FIRST)
    a_z.start(2, SECOND)
    expand(192, 128)
    b_y.start(2)
    a_z.start(3, FIRST)
    a_z.start(3, SECOND)
    expand(320, 128)
    b_y.arrived(1)
    a_z.start(4)
    expand(448, 256)
    contract(448, 256)
    a_z.arrived(3)
    expand(704, 128)
    contract(704, 128)
    b_y.arrived(2)
    expand(896, 128)
    contract(896, 128)
    s_by.first()
    a_z.arrived(4)
    expand(832, 64)
    contract(832, 64)
    s_az.first()
    contract(192, 256)
    contract(0, 192)
    s_az.advance(1)
    s_az.advance(2, FIRST)
    s_by.advance(1)
    s_az.advance(2, SECOND)
    s_az.advance(3, FIRST)
    s_by.advance(2, FIRST)
    s_az.advance(3, SECOND)
    s_az.advance(4, FIRST)
    s_by.advance(2, SECOND)
    s_bz.first()
    s_bz.advance(1)
    s_az.advance(4, SECOND)
    s_ay.first()
    s_bz.advance(2)
    s_ay.advance(1)
    s_bz.advance(3)
    s_ay.advance(2)

    c_x = Gather(NX, x, lambda p: device(p, y, z, core), *ring_sems(12), lambda r, h: mixed.at[
        (x + r + NX) % NX, pl.ds(h * short, short), :])
    rings.append(c_x)
    low, high = pl.ds(0, short), pl.ds(short, short)
    mixed[x, low, :] = (hidden_ref[low, :] + sums[slot_a, :].astype(F32)).astype(BF16)
    c_x.hop(1, 0, 0)
    c_x.hop(1, 0, 1)
    s_bz.advance(4)
    mixed[x, high, :] = (hidden_ref[high, :] + sums[slot_b, :].astype(F32)).astype(BF16)
    c_x.hop(1, 1, 1)
    c_x.hop(1, 1, 0)
    out_ref[here, :] = mixed[x]
    c_x.start(2)
    c_x.arrived(1)
    for r in (-1, 1):
        near = (x + r + NX) % NX
        out_ref[rows(near * few, few), :] = mixed[near]
    c_x.arrived(2)
    near = (x + 2) % NX
    out_ref[rows(near * few, few), :] = mixed[near]
    for c in pending:
        c.wait_send()
    for ring in rings:
        ring.drain()
    for _, _, c in lanes:
        c.wait_send()


def short_phase(a_y, b_z, a_z, b_y):
    a_y.start(1)
    b_z.start(1)
    a_y.start(2)
    b_z.start(2)
    a_y.arrived(1)
    a_y.arrived(2)
    a_z.start(1)
    b_z.start(3)
    b_z.start(4)
    for k in (1, 2, 3, 4):
        b_z.arrived(k)
    b_y.start(1)


def local(
    context, residual, branch_out_proj, norm_gain, router, expert_ids, gate_proj, up_proj, down_proj
):
    token_count, features = residual.shape
    few = token_count // NX
    half = few // 2
    width = gate_proj.shape[2]
    tall, wide = branch_out_proj.shape[1] // 2, branch_out_proj.shape[2] // 2
    vmem, hbm = pl.BlockSpec(memory_space=pltpu.VMEM), pl.BlockSpec(memory_space=pl.ANY)
    dma = pltpu.SemaphoreType.DMA
    plane = NY * NZ * few
    return pl.pallas_call(
        layer_kernel,
        out_shape=jax.ShapeDtypeStruct((token_count, features), BF16),
        in_specs=[vmem, hbm] + [vmem] * 4 + [hbm] * 3,
        out_specs=vmem,
        scratch_shapes=[
            pltpu.VMEM((2 * token_count, features), BF16),
            pltpu.VMEM((3, tall, wide), BF16),
            pltpu.VMEM((NZ, NY * tall, wide), BF16),
            pltpu.VMEM((2 * token_count, wide), F32),
            pltpu.VMEM((2 * token_count, wide), BF16),
            pltpu.VMEM((2 * NX, few, wide), BF16),
            pltpu.VMEM((few, features), F32),
            pltpu.VMEM((plane, features + GATES), BF16),
            pltpu.VMEM((features, 4 * width), BF16),
            pltpu.VMEM((2 * width, features), BF16),
            pltpu.VMEM((256, 4 * width), F32),
            pltpu.VMEM((plane, 2 * width), BF16),
            pltpu.VMEM((plane, features), BF16),
            pltpu.VMEM((2, 4, NY * half, features), BF16),
            pltpu.VMEM((2, 2, NZ * half, features), BF16),
            pltpu.VMEM((2, 2, half, features), BF16),
            pltpu.VMEM((2, 4, half, features), BF16),
            pltpu.VMEM((NX, few, features), BF16),
            dma((4,)), dma((7,)), dma((7,)), dma((13, 2, 4, 2)), dma((13, 2, 4, 2)), dma((8,)), dma((8,)),
        ],
        compiler_params=pltpu.CompilerParams(
            collective_id=0, has_side_effects=True, vmem_limit_bytes=62 * 2**20
        ),
        name="layer",
    )(
        branch_out_proj[0], context, residual, norm_gain.reshape(1, features), router.T, expert_ids.T,
        gate_proj[0], up_proj[0], down_proj[0],
    )


def solution(mesh):
    placed = (
        P(("branch", "dp"), None),
        P(("branch", "dp"), None),
        P("branch", "dp", "mp"),
        P(),
        P(),
        P(("branch", "dp"), None),
        P("branch", None, "dp"),
        P("branch", None, "dp"),
        P("branch", "dp", None),
    )
    return jax.shard_map(
        local, mesh=mesh, in_specs=placed, out_specs=P(("branch", "dp"), None), check_vma=False
    )
```

```python
import jax
import jax.numpy as jnp
from jax import lax
from jax.experimental import pallas as pl
from jax.experimental.pallas import tpu as pltpu
from jax.sharding import PartitionSpec as P

NX, NY, NZ = 4, 4, 8
MESH = pl.DeviceIdType.MESH
F32, BF16 = jnp.float32, jnp.bfloat16
GATES = 128
FIRST, SECOND = 0, 1


def position():
    b, d, x = lax.axis_index("branch"), lax.axis_index("dp"), lax.axis_index("mp")
    return x, (d % 2) * 2 + b // 2, d // 2, b % 2


def device(x, y, z, core):
    return {"branch": (y % 2) * 2 + core, "dp": z * 2 + y // 2, "mp": x}


def rows(start, size):
    return pl.ds(pl.multiple_of(start, size), size)


class Ring:
    def __init__(self, n, me, at, send, recv):
        self.n, self.me, self.at, self.send_sem, self.recv_sem = n, me, at, send, recv
        self.sent = []

    def near(self, step):
        return (self.me + step + self.n) % self.n

    def copy(self, src, dst, k, h, way):
        return pltpu.make_async_remote_copy(
            src_ref=src,
            dst_ref=dst,
            send_sem=self.send_sem(way, k - 1, h),
            recv_sem=self.recv_sem(way, k - 1, h),
            device_id=self.at(self.near(1 if way == 0 else -1)),
            device_id_type=MESH,
        )

    def launch(self, k, h, way):
        self.copy(*self.ends(k, h, way), k, h, way).start()
        self.sent.append((k, h, way))

    def drain(self):
        for k, h, way in self.sent:
            self.copy(*self.ends(k, h, way), k, h, way).wait_send()


class Gather(Ring):
    def __init__(self, n, me, at, send, recv, block, sliding=False):
        super().__init__(n, me, at, send, recv)
        self.block, self.sliding, self.seen = block, sliding, set()

    def lanes(self, k, turn):
        if turn == SECOND and k == self.n // 2:
            return []
        return [(way if turn == FIRST else 1 - way, way) for way in (0, 1)]

    def hop(self, k, h, way):
        if k > 1:
            self.arrive(k - 1, h, way)
        self.launch(k, h, way)

    def ends(self, k, h, way):
        sign = -1 if way == 0 else 1
        src = self.block(sign * (k - 1), h)
        return src, self.block(sign * k, h) if self.sliding else src

    def start(self, k, turn=None):
        for t in (FIRST, SECOND) if turn is None else (turn,):
            for h, way in self.lanes(k, t):
                self.hop(k, h, way)

    def arrive(self, k, h, way):
        if (k, h, way) not in self.seen:
            self.seen.add((k, h, way))
            part = self.block(-k if way == 0 else k, h)
            self.copy(part, part, k, h, way).wait_recv()

    def arrived(self, k):
        for t in (FIRST, SECOND):
            for h, way in self.lanes(k, t):
                self.arrive(k, h, way)


class Scatter(Ring):
    def __init__(self, n, me, at, send, recv, block, landing):
        super().__init__(n, me, at, send, recv)
        self.block, self.landing = block, landing

    def ends(self, k, h, way):
        far = self.n // 2 - k + 1
        return self.block(far if way == 0 else -far, h), self.landing(way, k - 1, h)

    def put(self, k, h, way):
        self.launch(k, h, way)

    def near_terms(self):
        for way in (0, 1):
            self.put(2, 1 - way, way)

    def far_terms(self):
        for way in (0, 1):
            self.put(1, way, way)

    def advance(self, k, turn=None):
        for t in (FIRST, SECOND) if turn is None else (turn,):
            if k == 1 and t == FIRST:
                continue
            for way in (0, 1):
                h = 1 - way if t == FIRST else way
                arrived = self.landing(way, k - 1, h)
                self.copy(arrived, arrived, k, h, way).wait_recv()
                left = self.n // 2 - k
                mine = self.block(left if way == 0 else -left, h)
                add_into(mine, arrived)
                if left:
                    self.put(k + 1, h, way)


def greet(peers):
    barrier = pltpu.get_barrier_semaphore()
    for peer in peers:
        pl.semaphore_signal(barrier, inc=1, device_id=peer, device_id_type=MESH)
    pl.semaphore_wait(barrier, len(peers))


A_ROWS = {0: 0, 4: 64, -4: 64, -1: 256, 1: 320, -2: 384, 2: 448, -3: 768, 3: 832}
B_ROWS = {0: 128, -1: 512, 1: 640, 2: 896, -2: 896}


def layer_kernel(
    block_ref, context_ref, residual_ref, gain_ref, router_ref, ids_ref, gate_ref, up_ref, down_ref,
    out_ref,
    context_all, pieces, merged, total, part, parts, hidden_ref,
    tok, enter, leave, act, inner, sums, land_az, land_by, land_ay, land_bz,
    load_sem, pair_send, pair_recv, ring_send, ring_recv, lane_send, lane_recv,
):
    x, y, z, core = position()
    other = 1 - core
    half = y % 2
    base = y - half
    mate = base + 1 - half
    width = gate_ref.shape[1]
    tokens, features = context_ref.shape
    loads = []
    for i, (src, dst) in enumerate((
        (context_ref, context_all.at[pl.ds(0, tokens), :]),
        (gate_ref, enter.at[:, pl.ds(0, width)]),
        (up_ref, enter.at[:, pl.ds(width, width)]),
        (down_ref, leave.at[pl.ds(0, width), :]),
    )):
        c = pltpu.make_async_copy(src, dst, load_sem.at[i])
        c.start()
        loads.append(c)
    peers = [device(x, y, z, other), device(x, mate, z, core), device(x, mate, z, other)]
    far_side = (y + 1 + 2 * (1 - half)) % NY
    peers += [device(x, far_side, z, core), device(x, y, (z + 1) % NZ, core), device(x, y, (z + 7) % NZ, core)]
    for dx in (1, 2, 3):
        for c in (core, other):
            peers.append(device((x + dx) % NX, y, z, c))
    greet(peers)

    def pair_copy(i, src, dst, to):
        return pltpu.make_async_remote_copy(
            src_ref=src, dst_ref=dst, send_sem=pair_send.at[i], recv_sem=pair_recv.at[i],
            device_id=to, device_id_type=MESH,
        )

    tall, wide = block_ref.shape[0] // 2, block_ref.shape[1] // 2
    sibling = device(x, y, z, other)
    pending = []
    for i, (dy, dc) in enumerate(((0, 1), (1, 0), (1, 1))):
        to_half = half if dy == 0 else 1 - half
        to_core = core if dc == 0 else other
        pending.append(pair_copy(
            i, block_ref.at[rows(to_half * tall, tall), rows(to_core * wide, wide)], pieces.at[i],
            device(x, base + to_half, z, to_core),
        ))
    pending.append(pair_copy(3, context_ref, context_all.at[pl.ds(tokens, tokens), :], sibling))
    pending.append(pair_copy(4, gate_ref, enter.at[:, pl.ds(2 * width, width)], sibling))
    pending.append(pair_copy(5, up_ref, enter.at[:, pl.ds(3 * width, width)], sibling))
    pending.append(pair_copy(6, down_ref, leave.at[pl.ds(width, width), :], sibling))
    for c in pending[:4]:
        c.start()
    for c in pending[:3]:
        c.wait_recv()
    for c in pending[4:]:
        c.start()
    own = block_ref[rows(half * tall, tall), rows(core * wide, wide)].astype(F32)
    own = own + pieces[0].astype(F32) + pieces[1].astype(F32) + pieces[2].astype(F32)
    merged[z, rows(y * tall, tall), :] = (own * 0.25).astype(BF16)

    quarter = wide // 2

    def ring_sems(i):
        return (lambda way, k, h: ring_send.at[i, way, k, h]), (lambda way, k, h: ring_recv.at[i, way, k, h])

    at_y = lambda p: device(x, p, z, core)
    at_z = lambda p: device(x, y, p, core)
    near_y = lambda r: (y + r + NY) % NY
    near_z = lambda r: (z + r + NZ) % NZ
    piece = tall // 2
    a_y = Gather(NY, y, at_y, *ring_sems(0), lambda r, h: merged.at[
        z, rows(near_y(r) * tall + h * piece, piece), pl.ds(0, quarter)])
    b_z = Gather(NZ, z, at_z, *ring_sems(1), lambda r, h: merged.at[
        near_z(r), rows(y * tall + h * piece, piece), pl.ds(quarter, quarter)])
    a_z = Gather(NZ, z, at_z, *ring_sems(2), lambda r, h: merged.at[
        near_z(r), pl.ds(h * 2 * tall, 2 * tall), pl.ds(0, quarter)])
    b_y = Gather(NY, y, at_y, *ring_sems(3), lambda r, h: merged.at[
        pl.ds(h * 4, 4), rows(near_y(r) * tall, tall), pl.ds(quarter, quarter)])
    rings = [a_y, b_z, a_z, b_y]

    left, right = pl.ds(0, quarter), pl.ds(quarter, quarter)

    def project_a(r):
        i = near_z(r)
        total[:, left] += jnp.dot(
            context_all[:, rows(i * 4 * tall, 4 * tall)], merged[i, :, left], preferred_element_type=F32
        )

    def project_b(r):
        i = near_y(r)
        terms = [
            jnp.dot(
                context_all[:, rows(i * tall + k * 4 * tall, tall)], merged[k, rows(i * tall, tall), right],
                preferred_element_type=F32,
            ) for k in range(NZ)
        ]
        total[:, right] += sum(terms[1:], terms[0])

    total[...] = jnp.zeros_like(total)

    def ready_context():
        loads[0].wait()
        pending[3].wait_recv()

    order = interleave(gather_events(a_y, b_z, a_z, b_y, 1.8, 7.0, 2.7), [
        ("a0", {"ay"}, 0.5, ("a", 0), None),
        ("b0", {"bz"}, 0.8, ("b", 0), None),
        ("a1m", {"az1"}, 0.5, ("a", -1), None),
        ("a1p", {"az1"}, 0.5, ("a", 1), None),
        ("a2m", {"az2"}, 0.5, ("a", -2), None),
        ("a2p", {"az2"}, 0.5, ("a", 2), None),
        ("b1m", {"by1"}, 0.8, ("b", -1), None),
        ("b1p", {"by1"}, 0.8, ("b", 1), None),
        ("a3m", {"az3"}, 0.5, ("a", -3), None),
        ("a3p", {"az3"}, 0.5, ("a", 3), None),
        ("b2", {"by2"}, 0.8, ("b", 2), None),
        ("a4", {"az4"}, 0.5, ("a", 4), None),
    ])
    first_step = next(i for i, item in enumerate(order) if not callable(item))
    run_in_order(order[:first_step] + [ready_context] + order[first_step:], {"a": project_a, "b": project_b})

    part[...] = total[...].astype(BF16)
    few = tokens // NX
    parts[x * 2 + core] = part[rows(x * few, few), :]
    lanes = []
    for dx in (2, 1, 3, 0):
        for dc in range(2):
            if dx or dc:
                to_x = (x + dx) % NX
                c = pltpu.make_async_remote_copy(
                    src_ref=part.at[rows(to_x * few + dc * tokens, few), :],
                    dst_ref=parts.at[x * 2 + core],
                    send_sem=lane_send.at[dx * 2 + dc], recv_sem=lane_recv.at[dx * 2 + dc],
                    device_id=device(to_x, y, z, core if dc == 0 else other), device_id_type=MESH,
                )
                c.start()
                lanes.append((dx, dc, c))
    for dx, dc, c in lanes:
        land = parts.at[(x + NX - dx) % NX * 2 + (core if dc == 0 else other)]
        pltpu.make_async_remote_copy(
            src_ref=land, dst_ref=land,
            send_sem=lane_send.at[dx * 2 + dc], recv_sem=lane_recv.at[dx * 2 + dc],
            device_id=sibling, device_id_type=MESH,
        ).wait_recv()
    here = rows(x * few, few)
    squares = jnp.zeros((few, 1), F32)
    for j in range(2 * NX):
        columns = pl.ds(j * wide, wide)
        hidden = residual_ref[here, columns].astype(F32) + parts[j].astype(F32)
        hidden_ref[:, columns] = hidden
        squares = squares + jnp.sum(hidden * hidden, axis=-1, keepdims=True)
    inv_rms = lax.rsqrt(squares / features + 1e-05)
    short = few // 2
    slot_a = rows(A_ROWS[0] + y * short, short)
    slot_b = rows(B_ROWS[0] + z * short, short)
    logits = jnp.zeros((few, 4), F32)
    for j in range(2 * NX):
        columns = pl.ds(j * wide, wide)
        normed = (hidden_ref[:, columns] * inv_rms * gain_ref[:, columns].astype(F32)).astype(BF16)
        tok[slot_a, columns] = normed[:short]
        tok[slot_b, columns] = normed[short:]
        logits = logits + lax.dot_general(
            normed, router_ref[:, columns], (((1,), (1,)), ((), ())), preferred_element_type=F32
        )
    lane = lax.broadcasted_iota(jnp.int32, (few, GATES), 1)
    row = lax.broadcasted_iota(jnp.int32, (few, GATES), 0)
    expert = lane % 4
    scores = 1.0 / (1.0 + jnp.exp(-logits))
    score_lanes = jnp.zeros((few, GATES), F32)
    for e in range(4):
        score_lanes = jnp.where(expert == e, scores[:, e:e + 1], score_lanes)
    ids = ids_ref[...].astype(F32)
    mine = lane == row + x * few
    first, second = (
        jnp.sum(jnp.where(mine, ids[k:k + 1, :], 0.0), axis=-1, keepdims=True) == expert.astype(F32) for k in (0, 1)
    )
    once = lane < 4
    picked_first = jnp.sum(jnp.where(first & once, score_lanes, 0.0), axis=-1, keepdims=True)
    picked_second = jnp.sum(jnp.where(second & once, score_lanes, 0.0), axis=-1, keepdims=True)
    weight = jnp.where(first, picked_first, jnp.where(second, picked_second, 0.0))
    weight = weight / (picked_first + picked_second)
    high = weight.astype(BF16).astype(F32)
    mid = (weight - high).astype(BF16).astype(F32)
    low = weight - high - mid
    sent = jnp.where(lane < 4, high, jnp.where(lane < 8, mid, jnp.where(lane < 12, low, 0.0))).astype(BF16)
    tok[slot_a, pl.ds(features, GATES)] = sent[:short]
    tok[slot_b, pl.ds(features, GATES)] = sent[short:]

    cut = features // 2

    def token_part(h):
        return pl.ds(0, cut) if h == 0 else pl.ds(cut, cut + GATES)

    def columns_of(c):
        return pl.ds(c * cut, cut)

    def sum_part(c, h):
        return pl.ds(c * cut + h * (cut // 2), cut // 2)

    in_a = lambda p: rows(A_ROWS[0] + p * short, short)
    in_b = lambda p: rows(B_ROWS[0] + p * short, short)
    part_a = lambda r, h: pl.ds(A_ROWS[r] + h * 2 * short, 2 * short)
    part_b = lambda r, h: pl.ds(B_ROWS[r] + h * 4 * short, 4 * short)
    a_y = Gather(NY, y, at_y, *ring_sems(4), lambda r, h: tok.at[in_a(near_y(r)), token_part(h)])
    b_z = Gather(NZ, z, at_z, *ring_sems(5), lambda r, h: tok.at[in_b(near_z(r)), token_part(h)])
    a_z = Gather(NZ, z, at_z, *ring_sems(6), lambda r, h: tok.at[part_a(r, h), :], True)
    b_y = Gather(NY, y, at_y, *ring_sems(7), lambda r, h: tok.at[part_b(r, h), :], True)
    s_az, s_by, s_ay, s_bz, s_x = [], [], [], [], []
    for c in range(2):
        s_az.append(Scatter(
            NZ, z, at_z, *ring_sems(8 + 5 * c), lambda r, h, c=c: sums.at[part_a(r, h), columns_of(c)],
            lambda way, k, h, c=c: land_az.at[way, k, pl.ds(h * 2 * short, 2 * short), columns_of(c)]))
        s_by.append(Scatter(
            NY, y, at_y, *ring_sems(9 + 5 * c), lambda r, h, c=c: sums.at[part_b(r, h), columns_of(c)],
            lambda way, k, h, c=c: land_by.at[way, k, pl.ds(h * 4 * short, 4 * short), columns_of(c)]))
        s_ay.append(Scatter(
            NY, y, at_y, *ring_sems(10 + 5 * c), lambda r, h, c=c: sums.at[in_a(near_y(r)), sum_part(c, h)],
            lambda way, k, h, c=c: land_ay.at[way, k, :, sum_part(c, h)]))
        s_bz.append(Scatter(
            NZ, z, at_z, *ring_sems(11 + 5 * c), lambda r, h, c=c: sums.at[in_b(near_z(r)), sum_part(c, h)],
            lambda way, k, h, c=c: land_bz.at[way, k, :, sum_part(c, h)]))
        s_x.append(Gather(
            NX, x, lambda p: device(p, y, z, core), *ring_sems(12 + 5 * c),
            lambda r, h, c=c: out_ref.at[(x + r + NX) % NX, pl.ds(h * short, short), columns_of(c)]))
    rings += [a_y, b_z, a_z, b_y, *s_az, *s_by, *s_ay, *s_bz, *s_x]

    own_expert = half * 2 + core
    two_expert = half * 2 + other

    def experts(start_one, start_two):
        few_rows = 4 * short
        one, two = rows(start_one, few_rows), rows(start_two, few_rows)
        tile = 2 * width

        @pl.loop(0, 2)
        def _(n):
            columns = rows(n * tile, tile)
            both = jnp.concatenate([tok[one, pl.ds(0, features)], tok[two, pl.ds(0, features)]], axis=0)
            act[:, columns] = jnp.dot(both, enter[:, columns], preferred_element_type=F32)

        gates = jnp.concatenate([tok[one, pl.ds(features, GATES)], tok[two, pl.ds(features, GATES)]], axis=0)
        gates = gates.astype(F32)
        names = lax.broadcasted_iota(jnp.int32, gates.shape, 1) % 4
        for s, e in ((0, own_expert), (1, two_expert)):
            scale = jnp.sum(jnp.where(names == e, gates, 0.0), axis=-1, keepdims=True)
            g = act[:, pl.ds(2 * s * width, width)]
            u = act[:, pl.ds((2 * s + 1) * width, width)]
            inner[:, pl.ds(s * width, width)] = (g / (1.0 + jnp.exp(-g)) * u * scale).astype(BF16)

        @pl.loop(0, 2)
        def _(n):
            columns = rows(n * cut, cut)
            result = jnp.dot(inner[...], leave[:, columns], preferred_element_type=F32).astype(BF16)
            sums[one, columns] = result[:few_rows]
            sums[two, columns] = result[few_rows:]

    def ready_weights():
        for c in loads[1:]:
            c.wait()
        for c in pending[4:]:
            c.wait_recv()

    def send_terms(ring_pair, far):
        def action():
            for ring in ring_pair:
                ring.far_terms() if far else ring.near_terms()
        return action

    def finish(h, c):
        span = pl.ds(h * short, short)
        slot = slot_a if h == 0 else slot_b
        out_ref[x, span, columns_of(c)] = (
            hidden_ref[span, columns_of(c)] + sums[slot, columns_of(c)].astype(F32)
        ).astype(BF16)
        s_x[c].hop(1, h, h)
        s_x[c].hop(1, h, 1 - h)

    length = 4.3
    order = interleave(gather_events(a_y, b_z, a_z, b_y, 2.5, 11.0, 5.5), [
        ("b0", {"bz"}, length, ("u", 128, 192), None),
        ("a1", {"az1"}, length, ("u", 256, 320), None),
        ("b1f", {"by1f"}, length, ("u", 512, 704), None),
        ("a2", {"az2"}, length, ("u", 384, 448), None),
        ("b1", {"by1"}, length, ("u", 576, 640), send_terms(s_by, False)),
        ("a3", {"az3"}, length, ("u", 768, 832), send_terms(s_az, False)),
        ("b2", {"by2"}, length, ("u", 896, 960), send_terms(s_by, True)),
        ("a4", {"az4"}, length, ("u", 0, 64), send_terms(s_az, True)),
    ])
    first_step = next(i for i, item in enumerate(order) if not callable(item))
    run_in_order(order[:first_step] + [ready_weights] + order[first_step:], {"u": experts})

    events = []

    def at(time, c, name, *actions):
        def run():
            for action in actions:
                action()

        events.append((time, f"{name}_{c}", run))

    for c in range(2):
        az, by, ay, bz, sx = s_az[c], s_by[c], s_ay[c], s_bz[c], s_x[c]
        go = lambda ring, k, turn: lambda: ring.advance(k, turn)
        t = 55.0 + 2.7 * c
        at(t, c, "az2f", go(az, 2, FIRST))
        at(t + 5.5, c, "az3f", go(az, 3, FIRST))
        at(t + 8, c, "az1", go(az, 1, SECOND))
        at(t + 12, c, "az4f", go(az, 4, FIRST))
        at(t + 15, c, "az2s", go(az, 2, SECOND))
        at(t + 20, c, "az3s", go(az, 3, SECOND))
        at(t + 27, c, "az4s", go(az, 4, SECOND), ay.near_terms, ay.far_terms)
        at(t + 29, c, "ay2f", go(ay, 2, FIRST))
        at(t + 29.1, c, "ay1", go(ay, 1, SECOND))
        at(t + 31, c, "ay2s", go(ay, 2, SECOND), lambda c=c: finish(0, c))
        t = 52.0 + 5.4 * c
        at(t, c, "by2f", go(by, 2, FIRST))
        at(t + 9, c, "by1", go(by, 1, SECOND))
        at(t + 20, c, "by2s", go(by, 2, SECOND), bz.near_terms, bz.far_terms)
        at(t + 22, c, "bz2f", go(bz, 2, FIRST))
        at(t + 22.1, c, "bz1", go(bz, 1, SECOND))
        at(t + 23.5, c, "bz3f", go(bz, 3, FIRST))
        at(t + 23.6, c, "bz2s", go(bz, 2, SECOND))
        at(t + 25, c, "bz4f", go(bz, 4, FIRST))
        at(t + 25.1, c, "bz3s", go(bz, 3, SECOND))
        at(t + 27, c, "bz4s", go(bz, 4, SECOND), lambda c=c: finish(1, c))
        at(90.0 + 3 * c, c, "x2", lambda sx=sx: sx.start(2))
        at(92.0 + 3 * c, c, "x", lambda sx=sx: (sx.arrived(1), sx.arrived(2)))
    for action in interleave(events, []):
        action()
    for c in pending:
        c.wait_send()
    for ring in rings:
        ring.drain()
    for _, _, c in lanes:
        c.wait_send()


def add_into(mine, arrived):
    step = 16

    @pl.loop(0, mine.shape[0] // step)
    def _(i):
        band = rows(i * step, step)
        mine[band, :] = (mine[band, :].astype(F32) + arrived[band, :].astype(F32)).astype(BF16)


def interleave(events, tasks):
    events, tasks, done, now, order = sorted(events, key=lambda e: e[0]), list(tasks), set(), 0.0, []
    while events or tasks:
        ready = [task for task in tasks if done.issuperset(task[1])]
        if events and (events[0][0] <= now or not ready):
            time, name, action = events.pop(0)
            now = max(now, time)
            order.append(action)
            done.add(name)
        else:
            name, _, length, step, action = ready[0]
            tasks.remove(ready[0])
            order += [step] + ([action] if action else [])
            done.add(name)
            now += length
    return order


def run_in_order(order, bodies):
    steps, before = [], [[]]
    for item in order:
        if callable(item):
            before[-1].append(item)
        else:
            steps.append(item)
            before.append([])

    @pl.loop(0, len(steps))
    def _(s):
        for i, actions in enumerate(before[:-1]):
            if actions:
                @pl.when(s == i)
                def _():
                    for action in actions:
                        action()
        for kind, body in bodies.items():
            places = [i for i, step in enumerate(steps) if step[0] == kind]
            chosen = s == places[0]
            numbers = [jnp.int32(number) for number in steps[places[0]][1:]]
            for i in places[1:]:
                chosen = chosen | (s == i)
                numbers = [jnp.where(s == i, jnp.int32(new), old) for new, old in zip(steps[i][1:], numbers)]
            if len(bodies) == 1:
                body(*numbers)
            else:
                pl.when(chosen)(lambda: body(*numbers))

    for action in before[-1]:
        action()


def gather_events(a_y, b_z, a_z, b_y, short_hop, long_start, part):
    def ready_a():
        a_y.arrived(1)
        a_y.arrived(2)
        a_z.start(1)

    def ready_b():
        for k in (1, 2, 3, 4):
            b_z.arrived(k)
        b_y.start(1)

    a_y.start(1)
    b_z.start(1)
    ta, tb = 2 * short_hop + 0.5, long_start
    plan = [
        (short_hop, "ay2", lambda: a_y.start(2)),
        (short_hop + 0.2, "bz2", lambda: b_z.start(2)),
        (ta, "ay", ready_a),
        (tb * 0.55, "bz3", lambda: b_z.start(3)),
        (tb * 0.8, "bz4", lambda: b_z.start(4)),
        (tb, "bz", ready_b),
        (ta + part + 1, "az2f", lambda: a_z.start(2, FIRST)),
        (ta + 2 * part + 1, "az1", lambda: a_z.start(2, SECOND)),
        (ta + 3 * part + 1, "az3f", lambda: a_z.start(3, FIRST)),
        (ta + 4 * part + 1, "az2", lambda: a_z.start(3, SECOND)),
        (ta + 5 * part + 1, "az4f", lambda: a_z.start(4)),
        (ta + 6 * part + 1, "az3", lambda: a_z.arrived(3)),
        (ta + 7 * part + 1, "az4", lambda: a_z.arrived(4)),
        (tb + 2 * part + 1, "by1f", lambda: b_y.start(2)),
        (tb + 4 * part + 1, "by1", lambda: b_y.arrived(1)),
        (tb + 6 * part + 1, "by2", lambda: b_y.arrived(2)),
    ]
    return plan


def local(
    context, residual, branch_out_proj, norm_gain, router, expert_ids, gate_proj, up_proj, down_proj
):
    token_count, features = residual.shape
    few = token_count // NX
    half = few // 2
    width = gate_proj.shape[2]
    tall, wide = branch_out_proj.shape[1] // 2, branch_out_proj.shape[2] // 2
    vmem, hbm = pl.BlockSpec(memory_space=pltpu.VMEM), pl.BlockSpec(memory_space=pl.ANY)
    dma = pltpu.SemaphoreType.DMA
    plane = NY * NZ * few
    return pl.pallas_call(
        layer_kernel,
        out_shape=jax.ShapeDtypeStruct((NX, few, features), BF16),
        in_specs=[vmem, hbm] + [vmem] * 4 + [hbm] * 3,
        out_specs=vmem,
        scratch_shapes=[
            pltpu.VMEM((2 * token_count, features), BF16),
            pltpu.VMEM((3, tall, wide), BF16),
            pltpu.VMEM((NZ, NY * tall, wide), BF16),
            pltpu.VMEM((2 * token_count, wide), F32),
            pltpu.VMEM((2 * token_count, wide), BF16),
            pltpu.VMEM((2 * NX, few, wide), BF16),
            pltpu.VMEM((few, features), F32),
            pltpu.VMEM((plane, features + GATES), BF16),
            pltpu.VMEM((features, 4 * width), BF16),
            pltpu.VMEM((2 * width, features), BF16),
            pltpu.VMEM((token_count, 4 * width), F32),
            pltpu.VMEM((token_count, 2 * width), BF16),
            pltpu.VMEM((plane, features), BF16),
            pltpu.VMEM((2, 4, NY * half, features), BF16),
            pltpu.VMEM((2, 2, NZ * half, features), BF16),
            pltpu.VMEM((2, 2, half, features), BF16),
            pltpu.VMEM((2, 4, half, features), BF16),
            dma((4,)), dma((7,)), dma((7,)), dma((18, 2, 4, 2)), dma((18, 2, 4, 2)), dma((8,)), dma((8,)),
        ],
        compiler_params=pltpu.CompilerParams(
            collective_id=0, has_side_effects=True, vmem_limit_bytes=62 * 2**20
        ),
        name="layer",
    )(
        branch_out_proj[0], context, residual, norm_gain.reshape(1, features), router.T, expert_ids.T,
        gate_proj[0], up_proj[0], down_proj[0],
    ).reshape(token_count, features)


def solution(mesh):
    placed = (
        P(("branch", "dp"), None),
        P(("branch", "dp"), None),
        P("branch", "dp", "mp"),
        P(),
        P(),
        P(("branch", "dp"), None),
        P("branch", None, "dp"),
        P("branch", None, "dp"),
        P("branch", "dp", None),
    )
    return jax.shard_map(
        local, mesh=mesh, in_specs=placed, out_specs=P(("branch", "dp"), None), check_vma=False
    )
```

```python
import jax
import jax.numpy as jnp
from jax import lax
from jax.experimental import pallas as pl
from jax.experimental.pallas import tpu as pltpu
from jax.sharding import PartitionSpec as P

NX, NY, NZ = 4, 4, 8
MESH = pl.DeviceIdType.MESH
F32, BF16 = jnp.float32, jnp.bfloat16
GATES = 128
FIRST, SECOND = 0, 1


def position():
    b, d, x = lax.axis_index("branch"), lax.axis_index("dp"), lax.axis_index("mp")
    return x, (d % 2) * 2 + b // 2, d // 2, b % 2


def device(x, y, z, core):
    return {"branch": (y % 2) * 2 + core, "dp": z * 2 + y // 2, "mp": x}


def rows(start, size):
    return pl.ds(pl.multiple_of(start, size), size)


class Ring:
    def __init__(self, n, me, at, send, recv):
        self.n, self.me, self.at, self.send_sem, self.recv_sem = n, me, at, send, recv
        self.sent = []

    def near(self, step):
        return (self.me + step + self.n) % self.n

    def copy(self, src, dst, k, h, way):
        return pltpu.make_async_remote_copy(
            src_ref=src,
            dst_ref=dst,
            send_sem=self.send_sem(way, k - 1, h),
            recv_sem=self.recv_sem(way, k - 1, h),
            device_id=self.at(self.near(1 if way == 0 else -1)),
            device_id_type=MESH,
        )

    def launch(self, k, h, way):
        self.copy(*self.ends(k, h, way), k, h, way).start()
        self.sent.append((k, h, way))

    def drain(self):
        for k, h, way in self.sent:
            self.copy(*self.ends(k, h, way), k, h, way).wait_send()


class Gather(Ring):
    def __init__(self, n, me, at, send, recv, block, sliding=False):
        super().__init__(n, me, at, send, recv)
        self.block, self.sliding, self.seen = block, sliding, set()

    def lanes(self, k, turn):
        if turn == SECOND and k == self.n // 2:
            return []
        return [(way if turn == FIRST else 1 - way, way) for way in (0, 1)]

    def hop(self, k, h, way):
        if k > 1:
            self.arrive(k - 1, h, way)
        self.launch(k, h, way)

    def ends(self, k, h, way):
        sign = -1 if way == 0 else 1
        src = self.block(sign * (k - 1), h)
        return src, self.block(sign * k, h) if self.sliding else src

    def start(self, k, turn=None):
        for t in (FIRST, SECOND) if turn is None else (turn,):
            for h, way in self.lanes(k, t):
                self.hop(k, h, way)

    def arrive(self, k, h, way):
        if (k, h, way) not in self.seen:
            self.seen.add((k, h, way))
            part = self.block(-k if way == 0 else k, h)
            self.copy(part, part, k, h, way).wait_recv()

    def arrived(self, k):
        for t in (FIRST, SECOND):
            for h, way in self.lanes(k, t):
                self.arrive(k, h, way)


class Scatter(Ring):
    def __init__(self, n, me, at, send, recv, block, landing):
        super().__init__(n, me, at, send, recv)
        self.block, self.landing = block, landing

    def ends(self, k, h, way):
        far = self.n // 2 - k + 1
        return self.block(far if way == 0 else -far, h), self.landing(way, k - 1, h)

    def put(self, k, h, way):
        self.launch(k, h, way)

    def near_terms(self):
        for way in (0, 1):
            self.put(2, 1 - way, way)

    def far_terms(self):
        for way in (0, 1):
            self.put(1, way, way)

    def first_terms(self):
        self.far_terms()
        self.near_terms()

    def advance(self, k, turn=None):
        for t in (FIRST, SECOND) if turn is None else (turn,):
            if k == 1 and t == FIRST:
                continue
            for way in (0, 1):
                h = 1 - way if t == FIRST else way
                arrived = self.landing(way, k - 1, h)
                self.copy(arrived, arrived, k, h, way).wait_recv()
                left = self.n // 2 - k
                mine = self.block(left if way == 0 else -left, h)
                add_into(mine, arrived)
                if left:
                    self.put(k + 1, h, way)


def greet(peers):
    barrier = pltpu.get_barrier_semaphore()
    for peer in peers:
        pl.semaphore_signal(barrier, inc=1, device_id=peer, device_id_type=MESH)
    pl.semaphore_wait(barrier, len(peers))


A_ROWS = {0: 0, 4: 64, -4: 64, -1: 256, 1: 320, -2: 384, 2: 448, -3: 768, 3: 832}
B_ROWS = {0: 128, -1: 512, 1: 640, 2: 896, -2: 896}


def layer_kernel(
    block_ref, context_ref, residual_ref, gain_ref, router_ref, ids_ref, gate_ref, up_ref, down_ref,
    out_ref,
    context_all, pieces, merged, total, part, parts, hidden_ref,
    tok, enter, leave, act, inner, sums, land_az, land_by, land_ay, land_bz,
    load_sem, pair_send, pair_recv, ring_send, ring_recv, lane_send, lane_recv,
):
    x, y, z, core = position()
    other = 1 - core
    half = y % 2
    base = y - half
    mate = base + 1 - half
    width = gate_ref.shape[1]
    tokens, features = context_ref.shape
    loads = []
    for i, (src, dst) in enumerate((
        (context_ref, context_all.at[pl.ds(0, tokens), :]),
        (gate_ref, enter.at[:, pl.ds(0, width)]),
        (up_ref, enter.at[:, pl.ds(width, width)]),
        (down_ref, leave.at[pl.ds(0, width), :]),
    )):
        c = pltpu.make_async_copy(src, dst, load_sem.at[i])
        c.start()
        loads.append(c)
    peers = [device(x, y, z, other), device(x, mate, z, core), device(x, mate, z, other)]
    far_side = (y + 1 + 2 * (1 - half)) % NY
    peers += [device(x, far_side, z, core), device(x, y, (z + 1) % NZ, core), device(x, y, (z + 7) % NZ, core)]
    for dx in (1, 2, 3):
        for c in (core, other):
            peers.append(device((x + dx) % NX, y, z, c))
    greet(peers)

    def pair_copy(i, src, dst, to):
        return pltpu.make_async_remote_copy(
            src_ref=src, dst_ref=dst, send_sem=pair_send.at[i], recv_sem=pair_recv.at[i],
            device_id=to, device_id_type=MESH,
        )

    tall, wide = block_ref.shape[0] // 2, block_ref.shape[1] // 2
    sibling = device(x, y, z, other)
    pending = []
    for i, (dy, dc) in enumerate(((0, 1), (1, 0), (1, 1))):
        to_half = half if dy == 0 else 1 - half
        to_core = core if dc == 0 else other
        pending.append(pair_copy(
            i, block_ref.at[rows(to_half * tall, tall), rows(to_core * wide, wide)], pieces.at[i],
            device(x, base + to_half, z, to_core),
        ))
    pending.append(pair_copy(3, context_ref, context_all.at[pl.ds(tokens, tokens), :], sibling))
    pending.append(pair_copy(4, gate_ref, enter.at[:, pl.ds(2 * width, width)], sibling))
    pending.append(pair_copy(5, up_ref, enter.at[:, pl.ds(3 * width, width)], sibling))
    pending.append(pair_copy(6, down_ref, leave.at[pl.ds(width, width), :], sibling))
    for c in pending[:4]:
        c.start()
    for c in pending[:3]:
        c.wait_recv()
    for c in pending[4:]:
        c.start()
    own = block_ref[rows(half * tall, tall), rows(core * wide, wide)].astype(F32)
    own = own + pieces[0].astype(F32) + pieces[1].astype(F32) + pieces[2].astype(F32)
    merged[z, rows(y * tall, tall), :] = (own * 0.25).astype(BF16)

    quarter = wide // 2

    def ring_sems(i):
        return (lambda way, k, h: ring_send.at[i, way, k, h]), (lambda way, k, h: ring_recv.at[i, way, k, h])

    at_y = lambda p: device(x, p, z, core)
    at_z = lambda p: device(x, y, p, core)
    near_y = lambda r: (y + r + NY) % NY
    near_z = lambda r: (z + r + NZ) % NZ
    piece = tall // 2
    a_y = Gather(NY, y, at_y, *ring_sems(0), lambda r, h: merged.at[
        z, rows(near_y(r) * tall + h * piece, piece), pl.ds(0, quarter)])
    b_z = Gather(NZ, z, at_z, *ring_sems(1), lambda r, h: merged.at[
        near_z(r), rows(y * tall + h * piece, piece), pl.ds(quarter, quarter)])
    a_z = Gather(NZ, z, at_z, *ring_sems(2), lambda r, h: merged.at[
        near_z(r), pl.ds(h * 2 * tall, 2 * tall), pl.ds(0, quarter)])
    b_y = Gather(NY, y, at_y, *ring_sems(3), lambda r, h: merged.at[
        pl.ds(h * 4, 4), rows(near_y(r) * tall, tall), pl.ds(quarter, quarter)])
    rings = [a_y, b_z, a_z, b_y]

    left, right = pl.ds(0, quarter), pl.ds(quarter, quarter)

    def project_a(r):
        i = near_z(r)
        total[:, left] += jnp.dot(
            context_all[:, rows(i * 4 * tall, 4 * tall)], merged[i, :, left], preferred_element_type=F32
        )

    def project_b(r):
        i = near_y(r)
        terms = [
            jnp.dot(
                context_all[:, rows(i * tall + k * 4 * tall, tall)], merged[k, rows(i * tall, tall), right],
                preferred_element_type=F32,
            ) for k in range(NZ)
        ]
        total[:, right] += sum(terms[1:], terms[0])

    total[...] = jnp.zeros_like(total)

    def ready_context():
        loads[0].wait()
        pending[3].wait_recv()

    order = interleave(gather_events(a_y, b_z, a_z, b_y, 2.0, 9.0, 2.9), [
        ("a0", {"ay"}, 0.5, ("a", 0), None),
        ("b0", {"bz"}, 0.8, ("b", 0), None),
        ("a1m", {"az1"}, 0.5, ("a", -1), None),
        ("a1p", {"az1"}, 0.5, ("a", 1), None),
        ("a2m", {"az2"}, 0.5, ("a", -2), None),
        ("a2p", {"az2"}, 0.5, ("a", 2), None),
        ("b1m", {"by1"}, 0.8, ("b", -1), None),
        ("b1p", {"by1"}, 0.8, ("b", 1), None),
        ("a3m", {"az3"}, 0.5, ("a", -3), None),
        ("a3p", {"az3"}, 0.5, ("a", 3), None),
        ("b2", {"by2"}, 0.8, ("b", 2), None),
        ("a4", {"az4"}, 0.5, ("a", 4), None),
    ])
    first_step = next(i for i, item in enumerate(order) if not callable(item))
    run_in_order(order[:first_step] + [ready_context] + order[first_step:], {"a": project_a, "b": project_b})

    part[...] = total[...].astype(BF16)
    few = tokens // NX
    parts[x * 2 + core] = part[rows(x * few, few), :]
    lanes = []
    for dx in (2, 1, 3, 0):
        for dc in range(2):
            if dx or dc:
                to_x = (x + dx) % NX
                c = pltpu.make_async_remote_copy(
                    src_ref=part.at[rows(to_x * few + dc * tokens, few), :],
                    dst_ref=parts.at[x * 2 + core],
                    send_sem=lane_send.at[dx * 2 + dc], recv_sem=lane_recv.at[dx * 2 + dc],
                    device_id=device(to_x, y, z, core if dc == 0 else other), device_id_type=MESH,
                )
                c.start()
                lanes.append((dx, dc, c))
    for dx, dc, c in lanes:
        land = parts.at[(x + NX - dx) % NX * 2 + (core if dc == 0 else other)]
        pltpu.make_async_remote_copy(
            src_ref=land, dst_ref=land,
            send_sem=lane_send.at[dx * 2 + dc], recv_sem=lane_recv.at[dx * 2 + dc],
            device_id=sibling, device_id_type=MESH,
        ).wait_recv()
    here = rows(x * few, few)
    squares = jnp.zeros((few, 1), F32)
    for j in range(2 * NX):
        columns = pl.ds(j * wide, wide)
        hidden = residual_ref[here, columns].astype(F32) + parts[j].astype(F32)
        hidden_ref[:, columns] = hidden
        squares = squares + jnp.sum(hidden * hidden, axis=-1, keepdims=True)
    inv_rms = lax.rsqrt(squares / features + 1e-05)
    short = few // 2
    slot_a = rows(A_ROWS[0] + y * short, short)
    slot_b = rows(B_ROWS[0] + z * short, short)
    logits = jnp.zeros((few, 4), F32)
    for j in range(2 * NX):
        columns = pl.ds(j * wide, wide)
        normed = (hidden_ref[:, columns] * inv_rms * gain_ref[columns].astype(F32)[None, :]).astype(BF16)
        tok[slot_a, columns] = normed[:short]
        tok[slot_b, columns] = normed[short:]
        logits = logits + lax.dot_general(
            normed, router_ref[:, columns], (((1,), (1,)), ((), ())), preferred_element_type=F32
        )
    lane = lax.broadcasted_iota(jnp.int32, (few, GATES), 1)
    row = lax.broadcasted_iota(jnp.int32, (few, GATES), 0)
    expert = lane % 4
    scores = 1.0 / (1.0 + jnp.exp(-logits))
    score_lanes = jnp.zeros((few, GATES), F32)
    for e in range(4):
        score_lanes = jnp.where(expert == e, scores[:, e:e + 1], score_lanes)
    ids = ids_ref[...].astype(F32)
    mine = lane == row + x * few
    first, second = (
        jnp.sum(jnp.where(mine, ids[k:k + 1, :], 0.0), axis=-1, keepdims=True) == expert.astype(F32) for k in (0, 1)
    )
    once = lane < 4
    picked_first = jnp.sum(jnp.where(first & once, score_lanes, 0.0), axis=-1, keepdims=True)
    picked_second = jnp.sum(jnp.where(second & once, score_lanes, 0.0), axis=-1, keepdims=True)
    weight = jnp.where(first, picked_first, jnp.where(second, picked_second, 0.0))
    weight = weight / (picked_first + picked_second)
    high = weight.astype(BF16).astype(F32)
    mid = (weight - high).astype(BF16).astype(F32)
    low = weight - high - mid
    sent = jnp.where(lane < 4, high, jnp.where(lane < 8, mid, jnp.where(lane < 12, low, 0.0))).astype(BF16)
    tok[slot_a, pl.ds(features, GATES)] = sent[:short]
    tok[slot_b, pl.ds(features, GATES)] = sent[short:]

    cut = features // 2

    def token_part(h):
        return pl.ds(0, cut) if h == 0 else pl.ds(cut, cut + GATES)

    def sum_part(h):
        return pl.ds(h * cut, cut)

    in_a = lambda p: rows(A_ROWS[0] + p * short, short)
    in_b = lambda p: rows(B_ROWS[0] + p * short, short)
    part_a = lambda r, h: pl.ds(A_ROWS[r] + h * 2 * short, 2 * short)
    part_b = lambda r, h: pl.ds(B_ROWS[r] + h * 4 * short, 4 * short)
    a_y = Gather(NY, y, at_y, *ring_sems(4), lambda r, h: tok.at[in_a(near_y(r)), token_part(h)])
    b_z = Gather(NZ, z, at_z, *ring_sems(5), lambda r, h: tok.at[in_b(near_z(r)), token_part(h)])
    a_z = Gather(NZ, z, at_z, *ring_sems(6), lambda r, h: tok.at[part_a(r, h), :], True)
    b_y = Gather(NY, y, at_y, *ring_sems(7), lambda r, h: tok.at[part_b(r, h), :], True)
    s_az = Scatter(NZ, z, at_z, *ring_sems(8), lambda r, h: sums.at[part_a(r, h), :],
                   lambda way, k, h: land_az.at[way, k, pl.ds(h * 2 * short, 2 * short), :])
    s_by = Scatter(NY, y, at_y, *ring_sems(9), lambda r, h: sums.at[part_b(r, h), :],
                   lambda way, k, h: land_by.at[way, k, pl.ds(h * 4 * short, 4 * short), :])
    s_ay = Scatter(NY, y, at_y, *ring_sems(10), lambda r, h: sums.at[in_a(near_y(r)), sum_part(h)],
                   lambda way, k, h: land_ay.at[way, k, :, sum_part(h)])
    s_bz = Scatter(NZ, z, at_z, *ring_sems(11), lambda r, h: sums.at[in_b(near_z(r)), sum_part(h)],
                   lambda way, k, h: land_bz.at[way, k, :, sum_part(h)])
    s_x = Gather(NX, x, lambda p: device(p, y, z, core), *ring_sems(12), lambda r, h: out_ref.at[
        (x + r + NX) % NX, pl.ds(h * short, short), :])
    rings += [a_y, b_z, a_z, b_y, s_az, s_by, s_ay, s_bz, s_x]

    own_expert = half * 2 + core
    two_expert = half * 2 + other

    def experts(start_one, start_two):
        few_rows = 4 * short
        one, two = rows(start_one, few_rows), rows(start_two, few_rows)
        tile = 2 * width

        @pl.loop(0, 2)
        def _(n):
            columns = rows(n * tile, tile)
            both = jnp.concatenate([tok[one, pl.ds(0, features)], tok[two, pl.ds(0, features)]], axis=0)
            act[:, columns] = jnp.dot(both, enter[:, columns], preferred_element_type=F32)

        gates = jnp.concatenate([tok[one, pl.ds(features, GATES)], tok[two, pl.ds(features, GATES)]], axis=0)
        gates = gates.astype(F32)
        names = lax.broadcasted_iota(jnp.int32, gates.shape, 1) % 4
        for s, e in ((0, own_expert), (1, two_expert)):
            scale = jnp.sum(jnp.where(names == e, gates, 0.0), axis=-1, keepdims=True)
            g = act[:, pl.ds(2 * s * width, width)]
            u = act[:, pl.ds((2 * s + 1) * width, width)]
            inner[:, pl.ds(s * width, width)] = (g / (1.0 + jnp.exp(-g)) * u * scale).astype(BF16)

        @pl.loop(0, 2)
        def _(n):
            columns = rows(n * cut, cut)
            result = jnp.dot(inner[...], leave[:, columns], preferred_element_type=F32).astype(BF16)
            sums[one, columns] = result[:few_rows]
            sums[two, columns] = result[few_rows:]

    def ready_weights():
        for c in loads[1:]:
            c.wait()
        for c in pending[4:]:
            c.wait_recv()

    def finish(h):
        span = pl.ds(h * short, short)
        slot = slot_a if h == 0 else slot_b
        out_ref[x, span, :] = (hidden_ref[span, :] + sums[slot, :].astype(F32)).astype(BF16)
        s_x.hop(1, h, h)
        s_x.hop(1, h, 1 - h)

    length = 4.3
    events = gather_events(a_y, b_z, a_z, b_y, 3.0, 14.5, 6.0)

    order = interleave(events, [
        ("b0", {"bz"}, length, ("u", 128, 192), None),
        ("a1", {"az1"}, length, ("u", 256, 320), None),
        ("b1f", {"by1f"}, length, ("u", 512, 704), None),
        ("a2", {"az2"}, length, ("u", 384, 448), None),
        ("b1", {"by1"}, length, ("u", 576, 640), None),
        ("a3", {"az3"}, length, ("u", 768, 832), None),
        ("b2", {"by2", "a3", "b1"}, length, ("u", 896, 960), s_by.first_terms),
        ("a4", {"az4", "b2"}, length, ("u", 0, 64), s_az.first_terms),
    ])
    first_step = next(i for i, item in enumerate(order) if not callable(item))
    run_in_order(order[:first_step] + [ready_weights] + order[first_step:], {"u": experts})
    s_az.advance(1)
    s_az.advance(2, FIRST)
    s_by.advance(1)
    s_az.advance(2, SECOND)
    s_az.advance(3, FIRST)
    s_by.advance(2, FIRST)
    s_az.advance(3, SECOND)
    s_az.advance(4, FIRST)


    s_by.advance(2, SECOND)
    s_bz.first_terms()
    s_bz.advance(1)
    s_bz.advance(2)
    s_az.advance(4, SECOND)
    s_ay.first_terms()
    s_bz.advance(3)
    s_ay.advance(1)
    s_bz.advance(4)
    finish(1)
    s_ay.advance(2)
    finish(0)
    s_x.start(2)
    s_x.arrived(1)
    s_x.arrived(2)
    for c in pending:
        c.wait_send()
    for ring in rings:
        ring.drain()
    for _, _, c in lanes:
        c.wait_send()


def add_into(mine, arrived):
    step = 16

    @pl.loop(0, mine.shape[0] // step)
    def _(i):
        band = rows(i * step, step)
        mine[band, :] = (mine[band, :].astype(F32) + arrived[band, :].astype(F32)).astype(BF16)


def interleave(events, tasks):
    events, tasks, done, now, order = sorted(events, key=lambda e: e[0]), list(tasks), set(), 0.0, []
    while events or tasks:
        ready = [task for task in tasks if done.issuperset(task[1])]
        if events and (events[0][0] <= now or not ready):
            time, name, action = events.pop(0)
            now = max(now, time)
            order.append(action)
            done.add(name)
        else:
            name, _, length, step, action = ready[0]
            tasks.remove(ready[0])
            order += [step] + ([action] if action else [])
            done.add(name)
            now += length
    return order


def run_in_order(order, bodies):
    steps, before = [], [[]]
    for item in order:
        if callable(item):
            before[-1].append(item)
        else:
            steps.append(item)
            before.append([])

    @pl.loop(0, len(steps))
    def _(s):
        for i, actions in enumerate(before[:-1]):
            if actions:
                @pl.when(s == i)
                def _():
                    for action in actions:
                        action()
        for kind, body in bodies.items():
            places = [i for i, step in enumerate(steps) if step[0] == kind]
            chosen = s == places[0]
            numbers = [jnp.int32(number) for number in steps[places[0]][1:]]
            for i in places[1:]:
                chosen = chosen | (s == i)
                numbers = [jnp.where(s == i, jnp.int32(new), old) for new, old in zip(steps[i][1:], numbers)]
            if len(bodies) == 1:
                body(*numbers)
            else:
                pl.when(chosen)(lambda: body(*numbers))

    for action in before[-1]:
        action()


def gather_events(a_y, b_z, a_z, b_y, short_hop, long_start, part):
    def ready_a():
        a_y.arrived(1)
        a_y.arrived(2)
        b_z.start(3)
        a_z.start(1, FIRST)

    def ready_b():
        for k in (1, 2, 3, 4):
            b_z.arrived(k)
        b_y.start(1)
        a_z.start(1, SECOND)

    a_y.start(1)
    b_z.start(1)
    late = long_start + 1
    plan = [
        (short_hop, "ay2", lambda: a_y.start(2)),
        (short_hop + 0.2, "bz2", lambda: b_z.start(2)),
        (2 * short_hop + 0.5, "ay", ready_a),
        (long_start * 0.8, "bz4", lambda: b_z.start(4)),
        (long_start, "bz", ready_b),
        (late, "az2f", lambda: a_z.start(2, FIRST)),
        (late + part, "az1", lambda: a_z.start(2, SECOND)),
        (late + 2 * part, "az3f", lambda: a_z.start(3, FIRST)),
        (late + 3 * part, "az2", lambda: a_z.start(3, SECOND)),
        (late + 4 * part, "az4f", lambda: a_z.start(4)),
        (late + 5 * part, "az3", lambda: a_z.arrived(3)),
        (late + 6 * part, "az4", lambda: a_z.arrived(4)),
        (long_start + 2 * part, "by1f", lambda: b_y.start(2)),
        (long_start + 4 * part, "by1", lambda: b_y.arrived(1)),
        (long_start + 6 * part, "by2", lambda: b_y.arrived(2)),
    ]
    return plan


def local(
    context, residual, branch_out_proj, norm_gain, router, expert_ids, gate_proj, up_proj, down_proj
):
    token_count, features = residual.shape
    few = token_count // NX
    half = few // 2
    width = gate_proj.shape[2]
    tall, wide = branch_out_proj.shape[1] // 2, branch_out_proj.shape[2] // 2
    vmem, hbm = pl.BlockSpec(memory_space=pltpu.VMEM), pl.BlockSpec(memory_space=pl.ANY)
    dma = pltpu.SemaphoreType.DMA
    plane = NY * NZ * few
    return pl.pallas_call(
        layer_kernel,
        out_shape=jax.ShapeDtypeStruct((NX, few, features), BF16),
        in_specs=[vmem, hbm] + [vmem] * 4 + [hbm] * 3,
        out_specs=vmem,
        scratch_shapes=[
            pltpu.VMEM((2 * token_count, features), BF16),
            pltpu.VMEM((3, tall, wide), BF16),
            pltpu.VMEM((NZ, NY * tall, wide), BF16),
            pltpu.VMEM((2 * token_count, wide), F32),
            pltpu.VMEM((2 * token_count, wide), BF16),
            pltpu.VMEM((2 * NX, few, wide), BF16),
            pltpu.VMEM((few, features), F32),
            pltpu.VMEM((plane, features + GATES), BF16),
            pltpu.VMEM((features, 4 * width), BF16),
            pltpu.VMEM((2 * width, features), BF16),
            pltpu.VMEM((token_count, 4 * width), F32),
            pltpu.VMEM((token_count, 2 * width), BF16),
            pltpu.VMEM((plane, features), BF16),
            pltpu.VMEM((2, 4, NY * half, features), BF16),
            pltpu.VMEM((2, 2, NZ * half, features), BF16),
            pltpu.VMEM((2, 2, half, features), BF16),
            pltpu.VMEM((2, 4, half, features), BF16),
            dma((4,)), dma((7,)), dma((7,)), dma((13, 2, 4, 2)), dma((13, 2, 4, 2)), dma((8,)), dma((8,)),
        ],
        compiler_params=pltpu.CompilerParams(
            collective_id=0, has_side_effects=True, vmem_limit_bytes=62 * 2**20
        ),
        name="layer",
    )(
        branch_out_proj[0], context, residual, norm_gain, router.T, expert_ids.T,
        gate_proj[0], up_proj[0], down_proj[0],
    ).reshape(token_count, features)


def solution(mesh):
    placed = (
        P(("branch", "dp"), None),
        P(("branch", "dp"), None),
        P("branch", "dp", "mp"),
        P(),
        P(),
        P(("branch", "dp"), None),
        P("branch", None, "dp"),
        P("branch", None, "dp"),
        P("branch", "dp", None),
    )
    return jax.shard_map(
        local, mesh=mesh, in_specs=placed, out_specs=P(("branch", "dp"), None), check_vma=False
    )
```

```python
import jax
import jax.numpy as jnp
from jax import lax
from jax.experimental import pallas as pl
from jax.experimental.pallas import tpu as pltpu
from jax.sharding import PartitionSpec as P

NX, NY, NZ = 4, 4, 8
MESH = pl.DeviceIdType.MESH
F32, BF16 = jnp.float32, jnp.bfloat16
GATES = 128
FIRST, SECOND = 0, 1


def position():
    b, d, x = lax.axis_index("branch"), lax.axis_index("dp"), lax.axis_index("mp")
    return x, (d % 2) * 2 + b // 2, d // 2, b % 2


def device(x, y, z, core):
    return {"branch": (y % 2) * 2 + core, "dp": z * 2 + y // 2, "mp": x}


def rows(start, size):
    return pl.ds(pl.multiple_of(start, size), size)


class Ring:
    def __init__(self, n, me, at, send, recv):
        self.n, self.me, self.at, self.send_sem, self.recv_sem = n, me, at, send, recv
        self.sent = []

    def near(self, step):
        return (self.me + step + self.n) % self.n

    def copy(self, src, dst, k, h, way):
        return pltpu.make_async_remote_copy(
            src_ref=src,
            dst_ref=dst,
            send_sem=self.send_sem(way, k - 1, h),
            recv_sem=self.recv_sem(way, k - 1, h),
            device_id=self.at(self.near(1 if way == 0 else -1)),
            device_id_type=MESH,
        )

    def launch(self, k, h, way):
        self.copy(*self.ends(k, h, way), k, h, way).start()
        self.sent.append((k, h, way))

    def drain(self):
        for k, h, way in self.sent:
            self.copy(*self.ends(k, h, way), k, h, way).wait_send()


class Gather(Ring):
    def __init__(self, n, me, at, send, recv, block, sliding=False):
        super().__init__(n, me, at, send, recv)
        self.block, self.sliding, self.seen = block, sliding, set()

    def lanes(self, k, turn):
        if turn == SECOND and k == self.n // 2:
            return []
        return [(way if turn == FIRST else 1 - way, way) for way in (0, 1)]

    def hop(self, k, h, way):
        if k > 1:
            self.arrive(k - 1, h, way)
        self.launch(k, h, way)

    def ends(self, k, h, way):
        sign = -1 if way == 0 else 1
        src = self.block(sign * (k - 1), h)
        return src, self.block(sign * k, h) if self.sliding else src

    def start(self, k, turn=None):
        for t in (FIRST, SECOND) if turn is None else (turn,):
            for h, way in self.lanes(k, t):
                self.hop(k, h, way)

    def arrive(self, k, h, way):
        if (k, h, way) not in self.seen:
            self.seen.add((k, h, way))
            part = self.block(-k if way == 0 else k, h)
            self.copy(part, part, k, h, way).wait_recv()

    def arrived(self, k):
        for t in (FIRST, SECOND):
            for h, way in self.lanes(k, t):
                self.arrive(k, h, way)


class Scatter(Ring):
    def __init__(self, n, me, at, send, recv, block, landing):
        super().__init__(n, me, at, send, recv)
        self.block, self.landing = block, landing

    def ends(self, k, h, way):
        far = self.n // 2 - k + 1
        return self.block(far if way == 0 else -far, h), self.landing(way, k - 1, h)

    def put(self, k, h, way):
        self.launch(k, h, way)

    def near_terms(self):
        for way in (0, 1):
            self.put(2, 1 - way, way)

    def far_terms(self):
        for way in (0, 1):
            self.put(1, way, way)

    def first_terms(self):
        self.far_terms()
        self.near_terms()

    def advance(self, k, turn=None):
        for t in (FIRST, SECOND) if turn is None else (turn,):
            if k == 1 and t == FIRST:
                continue
            for way in (0, 1):
                h = 1 - way if t == FIRST else way
                arrived = self.landing(way, k - 1, h)
                self.copy(arrived, arrived, k, h, way).wait_recv()
                left = self.n // 2 - k
                mine = self.block(left if way == 0 else -left, h)
                add_into(mine, arrived)
                if left:
                    self.put(k + 1, h, way)


def greet(peers):
    barrier = pltpu.get_barrier_semaphore()
    for peer in peers:
        pl.semaphore_signal(barrier, inc=1, device_id=peer, device_id_type=MESH)
    pl.semaphore_wait(barrier, len(peers))


A_ROWS = {0: 0, 4: 64, -4: 64, -1: 256, 1: 320, -2: 384, 2: 448, -3: 768, 3: 832}
B_ROWS = {0: 128, -1: 512, 1: 640, 2: 896, -2: 896}


def layer_kernel(
    block_ref, context_ref, residual_ref, gain_ref, router_ref, ids_ref, gate_ref, up_ref, down_ref,
    out_ref,
    context_all, pieces, merged, total, part, parts, hidden_ref,
    tok, enter, leave, act, inner, sums, land_az, land_by, land_ay, land_bz,
    load_sem, pair_send, pair_recv, ring_send, ring_recv, lane_send, lane_recv,
):
    x, y, z, core = position()
    other = 1 - core
    half = y % 2
    base = y - half
    mate = base + 1 - half
    width = gate_ref.shape[1]
    tokens, features = context_ref.shape
    loads = []
    for i, (src, dst) in enumerate((
        (context_ref, context_all.at[pl.ds(0, tokens), :]),
        (gate_ref, enter.at[:, pl.ds(0, width)]),
        (up_ref, enter.at[:, pl.ds(width, width)]),
        (down_ref, leave.at[pl.ds(0, width), :]),
    )):
        c = pltpu.make_async_copy(src, dst, load_sem.at[i])
        c.start()
        loads.append(c)
    peers = [device(x, y, z, other), device(x, mate, z, core), device(x, mate, z, other)]
    far_side = (y + 1 + 2 * (1 - half)) % NY
    peers += [device(x, far_side, z, core), device(x, y, (z + 1) % NZ, core), device(x, y, (z + 7) % NZ, core)]
    for dx in (1, 2, 3):
        for c in (core, other):
            peers.append(device((x + dx) % NX, y, z, c))
    greet(peers)

    def pair_copy(i, src, dst, to):
        return pltpu.make_async_remote_copy(
            src_ref=src, dst_ref=dst, send_sem=pair_send.at[i], recv_sem=pair_recv.at[i],
            device_id=to, device_id_type=MESH,
        )

    tall, wide = block_ref.shape[0] // 2, block_ref.shape[1] // 2
    sibling = device(x, y, z, other)
    pending = []
    for i, (dy, dc) in enumerate(((0, 1), (1, 0), (1, 1))):
        to_half = half if dy == 0 else 1 - half
        to_core = core if dc == 0 else other
        pending.append(pair_copy(
            i, block_ref.at[rows(to_half * tall, tall), rows(to_core * wide, wide)], pieces.at[i],
            device(x, base + to_half, z, to_core),
        ))
    pending.append(pair_copy(3, context_ref, context_all.at[pl.ds(tokens, tokens), :], sibling))
    pending.append(pair_copy(4, gate_ref, enter.at[:, pl.ds(2 * width, width)], sibling))
    pending.append(pair_copy(5, up_ref, enter.at[:, pl.ds(3 * width, width)], sibling))
    pending.append(pair_copy(6, down_ref, leave.at[pl.ds(width, width), :], sibling))
    for c in (pending[1], pending[2], pending[0], pending[3]):
        c.start()
    for c in pending[:3]:
        c.wait_recv()
    for c in pending[4:]:
        c.start()
    own = block_ref[rows(half * tall, tall), rows(core * wide, wide)].astype(F32)
    own = own + pieces[0].astype(F32) + pieces[1].astype(F32) + pieces[2].astype(F32)
    merged[z, rows(y * tall, tall), :] = (own * 0.25).astype(BF16)

    quarter = wide // 2

    def ring_sems(i):
        return (lambda way, k, h: ring_send.at[i, way, k, h]), (lambda way, k, h: ring_recv.at[i, way, k, h])

    at_y = lambda p: device(x, p, z, core)
    at_z = lambda p: device(x, y, p, core)
    near_y = lambda r: (y + r + NY) % NY
    near_z = lambda r: (z + r + NZ) % NZ
    piece = tall // 2
    a_y = Gather(NY, y, at_y, *ring_sems(0), lambda r, h: merged.at[
        z, rows(near_y(r) * tall + h * piece, piece), pl.ds(0, quarter)])
    b_z = Gather(NZ, z, at_z, *ring_sems(1), lambda r, h: merged.at[
        near_z(r), rows(y * tall + h * piece, piece), pl.ds(quarter, quarter)])
    a_z = Gather(NZ, z, at_z, *ring_sems(2), lambda r, h: merged.at[
        near_z(r), pl.ds(h * 2 * tall, 2 * tall), pl.ds(0, quarter)])
    b_y = Gather(NY, y, at_y, *ring_sems(3), lambda r, h: merged.at[
        pl.ds(h * 4, 4), rows(near_y(r) * tall, tall), pl.ds(quarter, quarter)])
    rings = [a_y, b_z, a_z, b_y]

    left, right = pl.ds(0, quarter), pl.ds(quarter, quarter)

    def project_a(r):
        i = near_z(r)
        total[:, left] += jnp.dot(
            context_all[:, rows(i * 4 * tall, 4 * tall)], merged[i, :, left], preferred_element_type=F32
        )

    def project_b(r):
        i = near_y(r)
        terms = [
            jnp.dot(
                context_all[:, rows(i * tall + k * 4 * tall, tall)], merged[k, rows(i * tall, tall), right],
                preferred_element_type=F32,
            ) for k in range(NZ)
        ]
        total[:, right] += sum(terms[1:], terms[0])

    total[...] = jnp.zeros_like(total)

    def ready_context():
        loads[0].wait()
        pending[3].wait_recv()

    order = interleave(gather_events(a_y, b_z, a_z, b_y, 2.0, 9.0, 2.9), [
        ("a0", {"ay"}, 0.5, ("a", 0), None),
        ("b0", {"bz"}, 0.8, ("b", 0), None),
        ("a1m", {"az1"}, 0.5, ("a", -1), None),
        ("a1p", {"az1"}, 0.5, ("a", 1), None),
        ("a2m", {"az2"}, 0.5, ("a", -2), None),
        ("a2p", {"az2"}, 0.5, ("a", 2), None),
        ("b1m", {"by1"}, 0.8, ("b", -1), None),
        ("b1p", {"by1"}, 0.8, ("b", 1), None),
        ("a3m", {"az3"}, 0.5, ("a", -3), None),
        ("a3p", {"az3"}, 0.5, ("a", 3), None),
        ("b2", {"by2"}, 0.8, ("b", 2), None),
        ("a4", {"az4"}, 0.5, ("a", 4), None),
    ])
    first_step = next(i for i, item in enumerate(order) if not callable(item))
    run_in_order(order[:first_step] + [ready_context] + order[first_step:], {"a": project_a, "b": project_b})

    part[...] = total[...].astype(BF16)
    few = tokens // NX
    parts[x * 2 + core] = part[rows(x * few, few), :]
    lanes = []
    for dx in (2, 1, 3, 0):
        for dc in range(2):
            if dx or dc:
                to_x = (x + dx) % NX
                c = pltpu.make_async_remote_copy(
                    src_ref=part.at[rows(to_x * few + dc * tokens, few), :],
                    dst_ref=parts.at[x * 2 + core],
                    send_sem=lane_send.at[dx * 2 + dc], recv_sem=lane_recv.at[dx * 2 + dc],
                    device_id=device(to_x, y, z, core if dc == 0 else other), device_id_type=MESH,
                )
                c.start()
                lanes.append((dx, dc, c))
    for dx, dc, c in lanes:
        land = parts.at[(x + NX - dx) % NX * 2 + (core if dc == 0 else other)]
        pltpu.make_async_remote_copy(
            src_ref=land, dst_ref=land,
            send_sem=lane_send.at[dx * 2 + dc], recv_sem=lane_recv.at[dx * 2 + dc],
            device_id=sibling, device_id_type=MESH,
        ).wait_recv()
    here = rows(x * few, few)
    squares = jnp.zeros((few, 1), F32)
    for j in range(2 * NX):
        columns = pl.ds(j * wide, wide)
        hidden = residual_ref[here, columns].astype(F32) + parts[j].astype(F32)
        hidden_ref[:, columns] = hidden
        squares = squares + jnp.sum(hidden * hidden, axis=-1, keepdims=True)
    inv_rms = lax.rsqrt(squares / features + 1e-05)
    short = few // 2
    slot_a = rows(A_ROWS[0] + y * short, short)
    slot_b = rows(B_ROWS[0] + z * short, short)
    logits = jnp.zeros((few, 4), F32)
    for j in range(2 * NX):
        columns = pl.ds(j * wide, wide)
        normed = (hidden_ref[:, columns] * inv_rms * gain_ref[columns].astype(F32)[None, :]).astype(BF16)
        tok[slot_a, columns] = normed[:short]
        tok[slot_b, columns] = normed[short:]
        logits = logits + lax.dot_general(
            normed, router_ref[:, columns], (((1,), (1,)), ((), ())), preferred_element_type=F32
        )
    lane = lax.broadcasted_iota(jnp.int32, (few, GATES), 1)
    row = lax.broadcasted_iota(jnp.int32, (few, GATES), 0)
    expert = lane % 4
    scores = 1.0 / (1.0 + jnp.exp(-logits))
    score_lanes = jnp.zeros((few, GATES), F32)
    for e in range(4):
        score_lanes = jnp.where(expert == e, scores[:, e:e + 1], score_lanes)
    ids = ids_ref[...].astype(F32)
    mine = lane == row + x * few
    first, second = (
        jnp.sum(jnp.where(mine, ids[k:k + 1, :], 0.0), axis=-1, keepdims=True) == expert.astype(F32) for k in (0, 1)
    )
    once = lane < 4
    picked_first = jnp.sum(jnp.where(first & once, score_lanes, 0.0), axis=-1, keepdims=True)
    picked_second = jnp.sum(jnp.where(second & once, score_lanes, 0.0), axis=-1, keepdims=True)
    weight = jnp.where(first, picked_first, jnp.where(second, picked_second, 0.0))
    weight = weight / (picked_first + picked_second)
    high = weight.astype(BF16).astype(F32)
    mid = (weight - high).astype(BF16).astype(F32)
    low = weight - high - mid
    sent = jnp.where(lane < 4, high, jnp.where(lane < 8, mid, jnp.where(lane < 12, low, 0.0))).astype(BF16)
    tok[slot_a, pl.ds(features, GATES)] = sent[:short]
    tok[slot_b, pl.ds(features, GATES)] = sent[short:]

    cut = features // 2

    def token_part(h):
        return pl.ds(0, cut) if h == 0 else pl.ds(cut, cut + GATES)

    def sum_part(h):
        return pl.ds(h * cut, cut)

    in_a = lambda p: rows(A_ROWS[0] + p * short, short)
    in_b = lambda p: rows(B_ROWS[0] + p * short, short)
    part_a = lambda r, h: pl.ds(A_ROWS[r] + h * 2 * short, 2 * short)
    part_b = lambda r, h: pl.ds(B_ROWS[r] + h * 4 * short, 4 * short)
    a_y = Gather(NY, y, at_y, *ring_sems(4), lambda r, h: tok.at[in_a(near_y(r)), token_part(h)])
    b_z = Gather(NZ, z, at_z, *ring_sems(5), lambda r, h: tok.at[in_b(near_z(r)), token_part(h)])
    a_z = Gather(NZ, z, at_z, *ring_sems(6), lambda r, h: tok.at[part_a(r, h), :], True)
    b_y = Gather(NY, y, at_y, *ring_sems(7), lambda r, h: tok.at[part_b(r, h), :], True)
    s_az = Scatter(NZ, z, at_z, *ring_sems(8), lambda r, h: sums.at[part_a(r, h), :],
                   lambda way, k, h: land_az.at[way, k, pl.ds(h * 2 * short, 2 * short), :])
    s_by = Scatter(NY, y, at_y, *ring_sems(9), lambda r, h: sums.at[part_b(r, h), :],
                   lambda way, k, h: land_by.at[way, k, pl.ds(h * 4 * short, 4 * short), :])
    s_ay = Scatter(NY, y, at_y, *ring_sems(10), lambda r, h: sums.at[in_a(near_y(r)), sum_part(h)],
                   lambda way, k, h: land_ay.at[way, k, :, sum_part(h)])
    s_bz = Scatter(NZ, z, at_z, *ring_sems(11), lambda r, h: sums.at[in_b(near_z(r)), sum_part(h)],
                   lambda way, k, h: land_bz.at[way, k, :, sum_part(h)])
    s_x = Gather(NX, x, lambda p: device(p, y, z, core), *ring_sems(12), lambda r, h: out_ref.at[
        (x + r + NX) % NX, pl.ds(h * short, short), :])
    rings += [a_y, b_z, a_z, b_y, s_az, s_by, s_ay, s_bz, s_x]

    own_expert = half * 2 + core
    two_expert = half * 2 + other

    def experts(start_one, start_two):
        few_rows = 4 * short
        one, two = rows(start_one, few_rows), rows(start_two, few_rows)
        tile = 2 * width

        @pl.loop(0, 2)
        def _(n):
            columns = rows(n * tile, tile)
            both = jnp.concatenate([tok[one, pl.ds(0, features)], tok[two, pl.ds(0, features)]], axis=0)
            act[:, columns] = jnp.dot(both, enter[:, columns], preferred_element_type=F32)

        gates = jnp.concatenate([tok[one, pl.ds(features, GATES)], tok[two, pl.ds(features, GATES)]], axis=0)
        gates = gates.astype(F32)
        names = lax.broadcasted_iota(jnp.int32, gates.shape, 1) % 4
        for s, e in ((0, own_expert), (1, two_expert)):
            scale = jnp.sum(jnp.where(names == e, gates, 0.0), axis=-1, keepdims=True)
            g = act[:, pl.ds(2 * s * width, width)]
            u = act[:, pl.ds((2 * s + 1) * width, width)]
            inner[:, pl.ds(s * width, width)] = (g / (1.0 + jnp.exp(-g)) * u * scale).astype(BF16)

        @pl.loop(0, 2)
        def _(n):
            columns = rows(n * cut, cut)
            result = jnp.dot(inner[...], leave[:, columns], preferred_element_type=F32).astype(BF16)
            sums[one, columns] = result[:few_rows]
            sums[two, columns] = result[few_rows:]

    def ready_weights():
        for c in loads[1:]:
            c.wait()
        for c in pending[4:]:
            c.wait_recv()

    def finish(h):
        span = pl.ds(h * short, short)
        slot = slot_a if h == 0 else slot_b
        out_ref[x, span, :] = (hidden_ref[span, :] + sums[slot, :].astype(F32)).astype(BF16)
        s_x.hop(1, h, h)
        s_x.hop(1, h, 1 - h)

    length = 4.3
    events = gather_events(a_y, b_z, a_z, b_y, 3.0, 14.5, 6.0)

    events.append((max(time for time, _, _ in events) + 5.0, "near", s_az.near_terms))
    order = interleave(events, [
        ("b0", {"bz"}, length, ("u", 128, 192), None),
        ("a1", {"az1"}, length, ("u", 256, 320), None),
        ("b1f", {"by1f"}, length, ("u", 512, 704), None),
        ("a2", {"az2"}, length, ("u", 384, 448), None),
        ("b1", {"by1"}, length, ("u", 576, 640), None),
        ("a3", {"az3"}, length, ("u", 768, 832), None),
        ("b2", {"by2", "a3", "b1"}, length, ("u", 896, 960), s_by.first_terms),
        ("a4", {"near", "b2"}, length, ("u", 0, 64), s_az.far_terms),
    ])
    first_step = next(i for i, item in enumerate(order) if not callable(item))
    run_in_order(order[:first_step] + [ready_weights] + order[first_step:], {"u": experts})
    s_az.advance(2, FIRST)
    s_az.advance(1)
    s_by.advance(1)
    s_az.advance(2, SECOND)
    s_az.advance(3, FIRST)
    s_by.advance(2, FIRST)
    s_az.advance(3, SECOND)
    s_az.advance(4, FIRST)


    s_by.advance(2, SECOND)
    s_bz.first_terms()
    s_bz.advance(1)
    s_bz.advance(2)
    s_az.advance(4, SECOND)
    s_ay.first_terms()
    s_bz.advance(3)
    s_ay.advance(1)
    s_bz.advance(4)
    finish(1)
    s_ay.advance(2)
    finish(0)
    s_x.start(2)
    s_x.arrived(1)
    s_x.arrived(2)
    for c in pending:
        c.wait_send()
    for ring in rings:
        ring.drain()
    for _, _, c in lanes:
        c.wait_send()


def add_into(mine, arrived):
    step = 16

    @pl.loop(0, mine.shape[0] // step)
    def _(i):
        band = rows(i * step, step)
        mine[band, :] = (mine[band, :].astype(F32) + arrived[band, :].astype(F32)).astype(BF16)


def interleave(events, tasks):
    events, tasks, done, now, order = sorted(events, key=lambda e: e[0]), list(tasks), set(), 0.0, []
    while events or tasks:
        ready = [task for task in tasks if done.issuperset(task[1])]
        if events and (events[0][0] <= now or not ready):
            time, name, action = events.pop(0)
            now = max(now, time)
            order.append(action)
            done.add(name)
        else:
            name, _, length, step, action = ready[0]
            tasks.remove(ready[0])
            order += [step] + ([action] if action else [])
            done.add(name)
            now += length
    return order


def run_in_order(order, bodies):
    steps, before = [], [[]]
    for item in order:
        if callable(item):
            before[-1].append(item)
        else:
            steps.append(item)
            before.append([])

    @pl.loop(0, len(steps))
    def _(s):
        for i, actions in enumerate(before[:-1]):
            if actions:
                @pl.when(s == i)
                def _():
                    for action in actions:
                        action()
        for kind, body in bodies.items():
            places = [i for i, step in enumerate(steps) if step[0] == kind]
            chosen = s == places[0]
            numbers = [jnp.int32(number) for number in steps[places[0]][1:]]
            for i in places[1:]:
                chosen = chosen | (s == i)
                numbers = [jnp.where(s == i, jnp.int32(new), old) for new, old in zip(steps[i][1:], numbers)]
            if len(bodies) == 1:
                body(*numbers)
            else:
                pl.when(chosen)(lambda: body(*numbers))

    for action in before[-1]:
        action()


def gather_events(a_y, b_z, a_z, b_y, short_hop, long_start, part):
    def ready_a():
        a_y.arrived(1)
        a_y.arrived(2)
        b_z.start(3)
        a_z.start(1, FIRST)

    def ready_b():
        for k in (1, 2, 3, 4):
            b_z.arrived(k)
        b_y.start(1)
        a_z.start(1, SECOND)

    a_y.start(1)
    b_z.start(1)
    late = long_start + 1
    plan = [
        (short_hop, "ay2", lambda: a_y.start(2)),
        (short_hop + 0.2, "bz2", lambda: b_z.start(2)),
        (2 * short_hop + 0.5, "ay", ready_a),
        (long_start * 0.8, "bz4", lambda: b_z.start(4)),
        (long_start, "bz", ready_b),
        (late, "az2f", lambda: a_z.start(2, FIRST)),
        (late + part, "az1", lambda: a_z.start(2, SECOND)),
        (late + 2 * part, "az3f", lambda: a_z.start(3, FIRST)),
        (late + 3 * part, "az2", lambda: a_z.start(3, SECOND)),
        (late + 4 * part, "az4f", lambda: a_z.start(4)),
        (late + 5 * part, "az3", lambda: a_z.arrived(3)),
        (late + 6 * part, "az4", lambda: a_z.arrived(4)),
        (long_start + 2 * part, "by1f", lambda: b_y.start(2)),
        (long_start + 4 * part, "by1", lambda: b_y.arrived(1)),
        (long_start + 6 * part, "by2", lambda: b_y.arrived(2)),
    ]
    return plan


def local(
    context, residual, branch_out_proj, norm_gain, router, expert_ids, gate_proj, up_proj, down_proj
):
    token_count, features = residual.shape
    few = token_count // NX
    half = few // 2
    width = gate_proj.shape[2]
    tall, wide = branch_out_proj.shape[1] // 2, branch_out_proj.shape[2] // 2
    vmem, hbm = pl.BlockSpec(memory_space=pltpu.VMEM), pl.BlockSpec(memory_space=pl.ANY)
    dma = pltpu.SemaphoreType.DMA
    plane = NY * NZ * few
    return pl.pallas_call(
        layer_kernel,
        out_shape=jax.ShapeDtypeStruct((NX, few, features), BF16),
        in_specs=[vmem, hbm] + [vmem] * 4 + [hbm] * 3,
        out_specs=vmem,
        scratch_shapes=[
            pltpu.VMEM((2 * token_count, features), BF16),
            pltpu.VMEM((3, tall, wide), BF16),
            pltpu.VMEM((NZ, NY * tall, wide), BF16),
            pltpu.VMEM((2 * token_count, wide), F32),
            pltpu.VMEM((2 * token_count, wide), BF16),
            pltpu.VMEM((2 * NX, few, wide), BF16),
            pltpu.VMEM((few, features), F32),
            pltpu.VMEM((plane, features + GATES), BF16),
            pltpu.VMEM((features, 4 * width), BF16),
            pltpu.VMEM((2 * width, features), BF16),
            pltpu.VMEM((token_count, 4 * width), F32),
            pltpu.VMEM((token_count, 2 * width), BF16),
            pltpu.VMEM((plane, features), BF16),
            pltpu.VMEM((2, 4, NY * half, features), BF16),
            pltpu.VMEM((2, 2, NZ * half, features), BF16),
            pltpu.VMEM((2, 2, half, features), BF16),
            pltpu.VMEM((2, 4, half, features), BF16),
            dma((4,)), dma((7,)), dma((7,)), dma((13, 2, 4, 2)), dma((13, 2, 4, 2)), dma((8,)), dma((8,)),
        ],
        compiler_params=pltpu.CompilerParams(
            collective_id=0, has_side_effects=True, vmem_limit_bytes=62 * 2**20
        ),
        name="layer",
    )(
        branch_out_proj[0], context, residual, norm_gain, router.T, expert_ids.T,
        gate_proj[0], up_proj[0], down_proj[0],
    ).reshape(token_count, features)


def solution(mesh):
    placed = (
        P(("branch", "dp"), None),
        P(("branch", "dp"), None),
        P("branch", "dp", "mp"),
        P(),
        P(),
        P(("branch", "dp"), None),
        P("branch", None, "dp"),
        P("branch", None, "dp"),
        P("branch", "dp", None),
    )
    return jax.shard_map(
        local, mesh=mesh, in_specs=placed, out_specs=P(("branch", "dp"), None), check_vma=False
    )
```
